32 devices in a mesh: groups: 2 (over y), cand: 4 (over z), tensor: 4 (over x, core).
Axes of the slice: x: 2, y: 2, z: 4, core: 2. Of those that a mesh axis runs over, the one named last changes fastest.
Arguments:
- response_latest_embeddings: bfloat16 [16, 384, 8192], P(('groups', 'cand'), None, 'tensor'), parts along dimension 0, may hold values from -6 to 6
- critic_probe_projector: bfloat16 [8192, 4096], P('cand', 'tensor'), may hold values from -0.0625 to 0.0625
- critic_pair_projector: bfloat16 [8192, 2048], P('cand', 'tensor'), may hold values from -0.0625 to 0.0625
- critic_stored_pairs: bfloat16 [16, 2048, 2048], P(('groups', 'cand'), None, 'tensor'), parts along dimension 0, may hold values from -1000 to 1000
- critic_grading_vector: float32 [4096], P('tensor'), may hold values from -6 to 6
- actor_stored_pairs: bfloat16 [16, 2048, 8, 256], P(('groups', 'cand'), None, 'tensor'), parts along dimension 0, may hold values from -1000 to 1000
- filled_extents: int32 [16], P('groups'), parts along dimension 0, may hold values from 1 to 2048, as said below
- kept_responses: int32 [8], P('groups'), parts along dimension 0, may hold values from 0 to 7, as said below
- actor_latest_probes: bfloat16 [8, 4, 4096], P(('groups', 'cand'), None, 'tensor'), parts along dimension 0, may hold values from -6 to 6
- actor_latest_pairs: bfloat16 [8, 4, 2048], P(('groups', 'cand'), None, 'tensor'), parts along dimension 0, may hold values from -6 to 6
Outputs:
- token_rewards: float32 [16, 384], P(('groups', 'cand')), parts along dimension 0
- actor_mixing_result: bfloat16 [8, 4, 4096], P(('groups', 'cand'), None, 'tensor'), parts along dimension 0
The draws below stay inside these ranges and needn't reach their ends.
There are 2 independent parts, one for each index of `groups`. The reference program is written for one: setup_inputs(seed, part) draws one part's arguments, and reference() takes and returns one part's arrays. A program takes and returns all parts, laid end to end along the dimension named above; an argument that names none is the same for every part. Nothing has to cross between parts.
Inputs may be any that keep to these rules, and one draw needn't show every extreme that they name: `kept_responses`: distinct candidate ids, always including 0 and 7. `filled_extents`: some candidate has exactly 2048 live tokens.
All inputs are finite; a program needn't handle non-finite values.
Results may differ from the reference program's by a relative error of at most 0.012.
The reference program's roundings to bfloat16 on the way count: a program that leaves them out, or rounds other values in their place, can miss the bound.
Values may be sent and summed in bfloat16 or wider, within the bound.
No kernel may reach another device: no remote copies, remote signals or barrier semaphores. Data moves between devices by JAX's collectives and lax.ppermute only.
A program may use at most 128 MiB of HBM per device.

```python
import jax
import jax.numpy as jnp
from jax import lax

D = 8192
RQH = 32
RKV = 8
HD = 128
PQH = 32
PKV = 8
CTX = 2048
SPAN = 384
PMAX = 2048
NEW = 4
CANDS = 8
KEEP = 4


def cache_entries(key, cands, length, heads):
    base = jnp.clip(jax.random.normal(key, (cands, length, heads, 2 * HD), jnp.float32), -6.0, 6.0)
    return base


def draw_critic_stored_pairs(key, part):
    values = cache_entries(jax.random.fold_in(key, 21), CANDS, CTX, RKV)
    return values.reshape(CANDS, CTX, RKV * 2 * HD).astype(jnp.bfloat16)


def draw_actor_stored_pairs(key, part):
    return cache_entries(jax.random.fold_in(key, 23), CANDS, PMAX, PKV).astype(jnp.bfloat16)


def draw_filled_extents(key, part):
    key_one, key_two = jax.random.split(jax.random.fold_in(key, 11))
    values = jax.random.randint(key_one, (CANDS,), 1, PMAX + 1)
    full_at = jax.random.randint(key_two, (), 0, CANDS)
    return values.at[full_at].set(PMAX).astype(jnp.int32)


def draw_kept_responses(key, part):
    key_one, key_two = jax.random.split(jax.random.fold_in(key, 13))
    middle = jax.random.permutation(key_one, jnp.arange(1, CANDS - 1, dtype=jnp.int32))[:KEEP - 2]
    chosen_lanes = jnp.concatenate([jnp.array([0, CANDS - 1], jnp.int32), middle])
    return jax.random.permutation(key_two, chosen_lanes).astype(jnp.int32)


def steps_of(rng, extent, cuts, smallest, top_value):
    def one(dim, parts):
        steps = jax.random.uniform(jax.random.fold_in(jax.random.fold_in(rng, 6), dim), (parts,), jnp.float32, smallest / len(cuts), top_value / len(cuts))
        return jnp.repeat(jnp.exp(steps), extent[dim] // parts).reshape((-1,) + (1,) * (len(extent) - dim - 1))

    loudness = one(*cuts[0])
    for cut in cuts[1:]:
        loudness = loudness * one(*cut)
    return loudness


def scatter_about(stream_key, dims, spread, most, cuts=(), kind=jnp.bfloat16):
    values = jax.random.normal(stream_key, dims, jnp.float32) * spread
    if len(cuts) > 0:
        values = steps_of(stream_key, dims, cuts, -0.22, 0.18) * values
    return jnp.clip(values, min=-most, max=most).astype(kind)


def setup_inputs(seed: int = 0, part: int = 0) -> dict:
    splits = jax.random.split(jax.random.key(seed), 11)
    part_keys = jax.random.split(jax.random.fold_in(splits[10], part), 11)
    return {
        "response_latest_embeddings": scatter_about(part_keys[0], (CANDS, SPAN, D), 1.0, 6.0, ((0, 4), (2, 4))),
        "critic_probe_projector": scatter_about(splits[1], (D, RQH * HD), D ** -0.5, 0.0625, ((0, 4), (1, 4))),
        "critic_pair_projector": scatter_about(splits[2], (D, RKV * 2 * HD), D ** -0.5, 0.0625, ((0, 4), (1, 4))),
        "critic_stored_pairs": draw_critic_stored_pairs(jax.random.fold_in(jax.random.fold_in(splits[10], part), 71), part),
        "critic_grading_vector": scatter_about(splits[4], (RQH * HD,), 1.0, 6.0, ((0, 4),), jnp.float32),
        "actor_stored_pairs": draw_actor_stored_pairs(jax.random.fold_in(jax.random.fold_in(splits[10], part), 71), part),
        "filled_extents": draw_filled_extents(jax.random.fold_in(jax.random.fold_in(splits[10], part), 71), part),
        "kept_responses": draw_kept_responses(jax.random.fold_in(jax.random.fold_in(splits[10], part), 71), part),
        "actor_latest_probes": scatter_about(part_keys[8], (KEEP, NEW, PQH * HD), 1.0, 6.0, ((0, 4), (2, 4))),
        "actor_latest_pairs": scatter_about(part_keys[9], (KEEP, NEW, PKV * 2 * HD), 1.0, 6.0, ((0, 4), (2, 4))),
    }


masked_value = -1e30


def reference(response_latest_embeddings, critic_probe_projector, critic_pair_projector, critic_stored_pairs, critic_grading_vector, actor_stored_pairs, filled_extents, kept_responses, actor_latest_probes, actor_latest_pairs):
    tok_rows = response_latest_embeddings.reshape(CANDS * SPAN, D)
    query_heads = jnp.dot(tok_rows, critic_probe_projector, preferred_element_type=jnp.float32).astype(jnp.bfloat16)
    keyval = jnp.dot(tok_rows, critic_pair_projector, preferred_element_type=jnp.float32).astype(jnp.bfloat16)
    query_heads = query_heads.reshape(CANDS, SPAN, RKV, RQH // RKV, HD)
    keyval = keyval.reshape(CANDS, SPAN, RKV, 2 * HD)
    cached = critic_stored_pairs.reshape(CANDS, CTX, RKV, 2 * HD)
    causal = jnp.arange(SPAN)[:, None] >= jnp.arange(SPAN)[None, :]
    visible = jnp.concatenate([jnp.ones((SPAN, CTX), dtype=bool), causal], axis=1)

    def score_one(entry_pair):
        queries, fresh_keys, old_keys = entry_pair
        every_key = jnp.concatenate([old_keys, fresh_keys], axis=0).astype(jnp.float32)
        scores = jnp.einsum("tkgd,skd->kgts", queries.astype(jnp.float32), every_key[..., :HD]) * HD ** -0.5
        scores = jnp.where(visible, scores, masked_value)
        rounded = lax.optimization_barrier(jax.nn.softmax(scores, axis=-1).astype(jnp.bfloat16))
        heads_out = jnp.einsum("kgts,skd->tkgd", rounded.astype(jnp.float32), every_key[..., HD:])
        return jnp.dot(heads_out.reshape(SPAN, RQH * HD), critic_grading_vector, precision=lax.Precision.HIGHEST)

    token_rewards = lax.map(score_one, (query_heads, keyval, cached))

    causal_new = jnp.arange(NEW)[:, None] >= jnp.arange(NEW)[None, :]

    def generate_for_lane(entry_pair):
        chosen_lanes, queries, fresh_keys = entry_pair
        old_keys = lax.dynamic_index_in_dim(actor_stored_pairs, chosen_lanes, 0, keepdims=False)
        live_len = lax.dynamic_index_in_dim(filled_extents, chosen_lanes, 0, keepdims=False)
        living_response_flags = jnp.arange(PMAX) < live_len
        visible_new = jnp.concatenate([jnp.broadcast_to(living_response_flags, (NEW, PMAX)), causal_new], axis=1)
        every_key = jnp.concatenate([old_keys, fresh_keys.reshape(NEW, PKV, 2 * HD)], axis=0).astype(jnp.float32)
        heads_in = queries.reshape(NEW, PKV, PQH // PKV, HD).astype(jnp.float32)
        scores = jnp.einsum("ikgd,skd->kgis", heads_in, every_key[..., :HD]) * HD ** -0.5
        scores = jnp.where(visible_new, scores, masked_value)
        weights = jax.nn.softmax(scores, axis=-1)
        heads_out = jnp.einsum("kgis,skd->ikgd", weights, every_key[..., HD:])
        return heads_out.reshape(NEW, PQH * HD).astype(jnp.bfloat16)

    actor_mixing_result = lax.map(generate_for_lane, (kept_responses, actor_latest_probes, actor_latest_pairs))
    return token_rewards, actor_mixing_result
```

```python
import math

import jax
import jax.numpy as jnp
from jax import lax
from jax.experimental import pallas as pl
from jax.experimental.pallas import tpu as pltpu
from jax.sharding import PartitionSpec as P

HD = 128
masked_value = -1e30
bf16, f32 = jnp.bfloat16, jnp.float32


def after(value, *earlier):
    return lax.optimization_barrier((value, *earlier))[0]


def shifted(value, axis, step):
    size = lax.axis_size(axis)
    return lax.ppermute(value, axis, [(i, (i + step) % size) for i in range(size)])


def partner(value, axis, bits):
    size = lax.axis_size(axis)
    return lax.ppermute(value, axis, [(i, i ^ bits) for i in range(size)])


def gather_rows(states, rows):
    tensor = lax.axis_size("tensor")
    here = lax.axis_index("tensor")
    share = states.reshape(rows, -1)
    width = share.shape[1]
    pieces = {(0, 0): share}
    far_bits = [1 << b for b in range(1, int(math.log2(tensor)))]
    for bit in reversed(far_bits[1:]):
        for (_, off), piece in list(pieces.items()):
            pieces[0, off ^ bit] = partner(piece, "tensor", bit)
    near = far_bits[0]
    half = rows // 2
    for (_, off), piece in list(pieces.items()):
        across = partner(piece, "tensor", near)
        other = partner(piece, "groups", 1)
        corner_low = partner(other[:half], "tensor", near)
        corner_high = partner(across[half:], "groups", 1)
        pieces[0, off ^ near] = across
        pieces[1, off] = other
        pieces[1, off ^ near] = jnp.concatenate([corner_low, corner_high], axis=0)
    for (group, off), piece in list(pieces.items()):
        pieces[group, off ^ 1] = partner(piece, "tensor", 1)
    whole = jnp.zeros((2 * rows, tensor * width), states.dtype)
    for (group, off), piece in pieces.items():
        whole = lax.dynamic_update_slice(whole, piece, (group * rows, (here ^ off) * width))
    return whole


def reward_kernel(kg_ref, q_ref, old_key_ref, old_value_ref, key_ref, value_ref, grade_ref, out_ref):
    span = q_ref.shape[0]
    context = old_key_ref.shape[1]
    rate = HD**-0.5 * math.log2(math.e)
    queries = q_ref[...]
    grade = grade_ref[0]
    block = math.gcd(512, context)
    peak = jnp.full((8, span), -jnp.inf, f32)
    total = jnp.zeros((8, span), f32)
    graded = jnp.zeros((8, span), f32)
    places = [(old_key_ref.at[0], old_value_ref.at[0], i, block) for i in range(0, context, block)]
    places.append((key_ref, value_ref, 0, span))
    for keys, values, start, size in places:
        scores = lax.dot_general(
            keys[start : start + size, :],
            queries,
            (((1,), (1,)), ((), ())),
            preferred_element_type=f32,
        )
        worth = jnp.dot(values[start : start + size, :], grade, preferred_element_type=f32)
        worth = worth[:, :HD] + worth[:, HD:]
        if keys is key_ref:
            shape = (size, span)
            visible = lax.broadcasted_iota(jnp.int32, shape, 0) <= lax.broadcasted_iota(
                jnp.int32, shape, 1
            )
            scores = jnp.where(visible, scores, masked_value)
        scores = scores.reshape(size // 8, 8, span)
        worth = worth.reshape(size // 8, 8, HD)
        new_peak = jnp.maximum(peak, jnp.max(scores, axis=0))
        fade = jnp.exp2((peak - new_peak) * rate)
        weights = jnp.exp2((scores - new_peak[None]) * rate)
        total = total * fade + jnp.sum(weights, axis=0)
        worth = jnp.concatenate([worth] * (span // HD), axis=2)
        graded = graded * fade + jnp.sum(weights * worth, axis=0)
        peak = new_peak
    top = jnp.max(peak, axis=0, keepdims=True)
    fade = jnp.exp2((peak - top) * rate)
    total = jnp.sum(total * fade, axis=0, keepdims=True)
    graded = jnp.sum(graded * fade, axis=0, keepdims=True)
    result = jnp.broadcast_to(graded / total, (8, span))

    @pl.when(pl.program_id(1) == 0)
    def _():
        out_ref[0] = result

    @pl.when(pl.program_id(1) != 0)
    def _():
        out_ref[0] += result


def grading_columns(grading):
    high = lax.reduce_precision(grading, 8, 7)
    parts = []
    for part in (high, grading - high):
        part = part.astype(bf16).reshape(-1, HD)
        parts.append(jnp.broadcast_to(part[:, :, None], (part.shape[0], HD, HD)))
    return jnp.concatenate(parts, axis=2)


def reward_share(queries, first_head, per_group, stored, fresh, grades):
    cands, context, _ = stored.shape
    span = queries.shape[0] // cands
    heads = queries.shape[1] // HD
    numbers = first_head + lax.broadcasted_iota(jnp.int32, (heads,), 0)
    groups = numbers // per_group
    grade = lax.dynamic_slice_in_dim(grades, first_head, heads, 0)
    spec = pltpu.PrefetchScalarGridSpec(
        num_scalar_prefetch=1,
        grid=(cands, heads),
        in_specs=[
            pl.BlockSpec((span, HD), lambda c, h, g: (c, h)),
            pl.BlockSpec((1, context, HD), lambda c, h, g: (c, 0, 2 * g[h])),
            pl.BlockSpec((1, context, HD), lambda c, h, g: (c, 0, 2 * g[h] + 1)),
            pl.BlockSpec((span, HD), lambda c, h, g: (c, 2 * g[h])),
            pl.BlockSpec((span, HD), lambda c, h, g: (c, 2 * g[h] + 1)),
            pl.BlockSpec((1, HD, 2 * HD), lambda c, h, g: (h, 0, 0)),
        ],
        out_specs=pl.BlockSpec((1, 8, span), lambda c, h, g: (c, 0, 0)),
    )
    cells = cands * heads * span * (context + span)
    share = pl.pallas_call(
        reward_kernel,
        grid_spec=spec,
        out_shape=jax.ShapeDtypeStruct((cands, 8, span), f32),
        compiler_params=pltpu.CompilerParams(vmem_limit_bytes=40 * 1024 * 1024),
        cost_estimate=pl.CostEstimate(
            flops=6 * HD * cells, bytes_accessed=4 * stored.size, transcendentals=cells
        ),
        name="reward_share",
    )(groups, queries, stored, stored, fresh, fresh, grade)
    return share[:, 0, :]


def policy(stored, extents, kept, probes, pairs):
    cand_here = stored.shape[0]
    device_here = lax.axis_index("cand")
    devices = lax.axis_size("cand")
    key_scale = HD ** (-0.5)
    slots_here = probes.shape[0]
    lane_number = kept.shape[0]
    new_count = probes.shape[1]
    kv_here = stored.shape[2]
    policy_heads = probes.shape[2] // HD
    policy_group = policy_heads // kv_here
    cache_len = stored.shape[1]
    own = jnp.concatenate([probes, pairs], axis=2)
    everyone = jnp.zeros((lane_number,) + own.shape[1:], own.dtype)
    for step in range(devices):
        part = shifted(own, "cand", step) if step else own
        at = (device_here - step) % devices * slots_here
        everyone = lax.dynamic_update_slice(everyone, part, (at, 0, 0))
    causal_new = lax.broadcasted_iota(jnp.int32, (new_count, new_count), 0) >= lax.broadcasted_iota(
        jnp.int32, (new_count, new_count), 1
    )
    ids_here = device_here * cand_here + lax.broadcasted_iota(jnp.int32, (cand_here,), 0)
    matched = kept[None, :] == ids_here[:, None]
    slot_index = jnp.sum(
        jnp.where(matched, lax.broadcasted_iota(jnp.int32, (cand_here, lane_number), 1), 0), axis=1
    )
    chosen = jnp.take(everyone, slot_index, axis=0)
    own_queries = chosen[:, :, : policy_heads * HD].reshape(
        cand_here, new_count, kv_here, policy_group, HD
    )
    own_fresh = chosen[:, :, policy_heads * HD :].reshape(cand_here, new_count, kv_here, 2 * HD)
    living = lax.broadcasted_iota(jnp.int32, (cand_here, cache_len), 1)
    living = living < jnp.take(extents, ids_here)[:, None]
    living = living[:, None, None, None, :]
    scores = (
        jnp.einsum("cikgd,ctkd->ckgit", own_queries, stored[..., :HD], preferred_element_type=f32)
        * key_scale
    )
    scores = jnp.where(living, scores, masked_value)
    fresh_scores = (
        jnp.einsum("cikgd,cjkd->ckgij", own_queries, own_fresh[..., :HD], preferred_element_type=f32)
        * key_scale
    )
    fresh_scores = jnp.where(causal_new, fresh_scores, masked_value)
    peak_score = jnp.maximum(jnp.max(scores, axis=-1), jnp.max(fresh_scores, axis=-1))
    old_weights = jnp.where(living, jnp.exp(scores - peak_score[..., None]), 0.0)
    fresh_weights = jnp.where(causal_new, jnp.exp(fresh_scores - peak_score[..., None]), 0.0)
    denominator = jnp.sum(old_weights, axis=-1) + jnp.sum(fresh_weights, axis=-1)
    numerator = jnp.einsum(
        "ckgit,ctkd->ckgid", old_weights, stored[..., HD:], preferred_element_type=f32
    )
    numerator = numerator + jnp.einsum(
        "ckgij,cjkd->ckgid", fresh_weights, own_fresh[..., HD:], preferred_element_type=f32
    )
    result = numerator / denominator[..., None]
    flattened = jnp.transpose(result, (0, 3, 1, 2, 4)).reshape(
        cand_here, new_count * policy_heads * HD
    )
    placed = jnp.einsum(
        "cs,cx->sx", matched.astype(f32), flattened, precision=lax.Precision.HIGHEST
    )
    placed = placed.reshape(lane_number, new_count, policy_heads * HD).astype(bf16)
    rows = jnp.zeros((slots_here,) + placed.shape[1:], f32)
    for step in range(devices):
        at = (device_here + step) % devices * slots_here
        part = lax.dynamic_slice_in_dim(placed, at, slots_here, 0)
        rows = rows + (shifted(part, "cand", step) if step else part).astype(f32)
    return rows.astype(bf16)


def local(
    response_latest_embeddings,
    critic_probe_projector,
    critic_pair_projector,
    critic_stored_pairs,
    critic_grading_vector,
    actor_stored_pairs,
    filled_extents,
    kept_responses,
    actor_latest_probes,
    actor_latest_pairs,
):
    cand_here, span_len, _ = response_latest_embeddings.shape
    rows = cand_here * span_len
    devices = lax.axis_size("cand")
    group = lax.axis_index("groups")
    place = lax.axis_index("cand")
    depth, query_cols = critic_probe_projector.shape
    keyval_cols = critic_pair_projector.shape[1]
    heads_here = query_cols // HD
    per_group = heads_here // (keyval_cols // (2 * HD))
    query_half, keyval_half = query_cols // 2, keyval_cols // 2

    heads_half = heads_here // 2
    cut = heads_half // 2
    chunks = [("keyval", 0, keyval_half), ("query", 0, cut * HD), ("query", cut * HD, query_half)]
    shares = []
    for kind, low, high in chunks:
        array, half = {
            "keyval": (critic_pair_projector, keyval_half),
            "query": (critic_probe_projector, query_half),
        }[kind]
        shares.append(lax.dynamic_slice(array, (0, group * half + low), (depth, high - low)))

    whole_rows = gather_rows(response_latest_embeddings, rows)

    rings = [[share] for share in shares]
    first, second, third = rings
    for step in range(devices - 1):
        first.append(shifted(first[-1], "cand", 1))
        second.append(shifted(second[-1], "cand", 1))
    third[0] = after(third[0], first[-1])
    for step in range(devices - 1):
        third.append(shifted(third[-1], "cand", 1))

    def project(ring):
        total = None
        for step, weights in enumerate(ring):
            columns = lax.dynamic_slice_in_dim(
                whole_rows, (place - step) % devices * depth, depth, 1
            )
            term = jnp.dot(columns, weights, preferred_element_type=f32)
            total = term if total is None else total + term
        total = total.astype(bf16)
        return total[:rows], partner(total[rows:], "groups", 1)

    results = [project(ring) for ring in rings]
    kept_keyval, sent_keyval = results[0]
    keyval = jnp.where(
        group == 0,
        jnp.concatenate([kept_keyval, sent_keyval], axis=1),
        jnp.concatenate([sent_keyval, kept_keyval], axis=1),
    )
    grades = grading_columns(critic_grading_vector)
    share = jnp.zeros((cand_here, span_len), f32)
    for (kind, low, _), (kept, sent) in zip(chunks[1:], results[1:]):
        for queries, owner in ((kept, group), (sent, 1 - group)):
            share = share + reward_share(
                queries,
                owner * heads_half + low // HD,
                per_group,
                critic_stored_pairs,
                keyval,
                grades,
            )
    tensor = lax.axis_size("tensor")
    terms = [share] + [partner(share, "tensor", bits) for bits in range(1, tensor)]
    while len(terms) > 1:
        terms = [a + b for a, b in zip(terms[::2], terms[1::2])]
    slot_rows = policy(
        actor_stored_pairs, filled_extents, kept_responses, actor_latest_probes, actor_latest_pairs
    )
    return terms[0], slot_rows


def solution(mesh):
    placed = (
        P(("groups", "cand"), None, "tensor"),
        P("cand", "tensor"),
        P("cand", "tensor"),
        P(("groups", "cand"), None, "tensor"),
        P("tensor"),
        P(("groups", "cand"), None, "tensor", None),
        P("groups"),
        P("groups"),
        P(("groups", "cand"), None, "tensor"),
        P(("groups", "cand"), None, "tensor"),
    )
    return jax.shard_map(
        local,
        mesh=mesh,
        in_specs=placed,
        out_specs=(P(("groups", "cand"), None), P(("groups", "cand"), None, "tensor")),
        check_vma=False,
    )
```

```python
import functools
import math

import jax
import jax.numpy as jnp
from jax import lax
from jax.experimental import pallas as pl
from jax.experimental.pallas import tpu as pltpu
from jax.sharding import PartitionSpec as P

HD = 128
masked_value = -1e30
bf16, f32 = jnp.bfloat16, jnp.float32


def after(value, *earlier):
    return lax.optimization_barrier((value, *earlier))[0]


def shifted(value, axis, step):
    size = lax.axis_size(axis)
    return lax.ppermute(value, axis, [(i, (i + step) % size) for i in range(size)])


def partner(value, axis, bits):
    size = lax.axis_size(axis)
    return lax.ppermute(value, axis, [(i, i ^ bits) for i in range(size)])


def gather_rows(states, rows):
    tensor = lax.axis_size("tensor")
    share = states.reshape(rows, -1)
    half = rows // 2
    own, other = {0: share}, {}
    far_bits = [1 << b for b in range(1, int(math.log2(tensor)))]
    for bit in reversed(far_bits[1:]):
        for off, piece in list(own.items()):
            own[off ^ bit] = partner(piece, "tensor", bit)
    near = far_bits[0]
    corners = {}
    for off, piece in list(own.items()):
        across = partner(piece, "tensor", near)
        other[off] = partner(piece, "groups", 1)
        low = partner(other[off][:half], "tensor", near)
        high = partner(across[half:], "groups", 1)
        own[off ^ near] = across
        corners[off ^ near] = (low, high)
    for pieces in (own, other):
        for off, piece in list(pieces.items()):
            pieces[off ^ 1] = partner(piece, "tensor", 1)
    for off, (low, high) in list(corners.items()):
        corners[off ^ 1] = (partner(low, "tensor", 1), partner(high, "tensor", 1))
    tiles = [[], [], [], []]
    for off in range(tensor):
        low, high = corners.get(off, (None, None))
        tiles[0].append((own[off], 0))
        tiles[1].append((own[off], half))
        tiles[2].append((other[off], 0) if low is None else (low, 0))
        tiles[3].append((other[off], half) if low is None else (high, 0))
    return tiles


def project_kernel(plan, where_ref, *refs):
    sources, tile_of, blocks, widths, has_sum, final = plan
    arrays, refs = refs[:sources], refs[sources:]
    weights, refs = refs[: blocks * len(widths)], refs[blocks * len(widths) :]
    before, refs = (refs[0], refs[1:]) if has_sum else (None, refs)
    out, (tile_buf, weight_buf, sum_buf, tile_sem, weight_sem, sum_sem) = refs[0], refs[1:]
    tile_rows, depth = tile_buf.shape[1:]
    slots = tile_buf.shape[0]
    steps = 4 * blocks

    def load(item):
        block, tile = item // 4, item % 4
        off, column = where_ref[2 * block], where_ref[2 * block + 1]
        column = pl.multiple_of(column, depth)
        slot = lax.rem(item, slots)
        for i, row in enumerate(tile_of):
            for j, (number, start) in enumerate(row):

                @pl.when((tile == i) & (off == j))
                def _():
                    pltpu.make_async_copy(
                        arrays[number].at[pl.ds(start, tile_rows), pl.ds(column, depth)],
                        tile_buf.at[slot],
                        tile_sem.at[slot],
                    ).start()

    copies = []
    for block in range(blocks):
        at = 0
        for j, width in enumerate(widths):
            number = block * len(widths) + j
            copies.append(
                pltpu.make_async_copy(
                    weights[number],
                    weight_buf.at[block, :, at : at + width],
                    weight_sem.at[number],
                )
            )
            at += width
    first = len(widths)
    for copy in copies[:first]:
        copy.start()
    for item in range(slots - 1):
        load(item)
    for copy in copies[first:]:
        copy.start()
    if has_sum:
        sum_copy = pltpu.make_async_copy(before, sum_buf, sum_sem)
        sum_copy.start()
        sum_copy.wait()
    for copy in copies:
        copy.wait()

    def step(item, _):
        @pl.when(item + slots - 1 < steps)
        def _():
            load(item + slots - 1)

        slot = lax.rem(item, slots)
        block, tile = item // 4, item % 4
        pltpu.make_async_copy(
            arrays[0].at[pl.ds(0, tile_rows), pl.ds(0, depth)], tile_buf.at[slot], tile_sem.at[slot]
        ).wait()
        term = jnp.dot(tile_buf[slot], weight_buf[block], preferred_element_type=f32)
        if has_sum:
            term = term + sum_buf[tile]
        else:
            term = jnp.where(block > 0, term + sum_buf[tile], term)
        if final:

            @pl.when(block == blocks - 1)
            def _():
                out[tile] = term.astype(bf16)

        if not final or blocks > 1:
            sum_buf[tile] = term
        return 0

    lax.fori_loop(0, steps, step, 0)
    if not final:
        out[...] = sum_buf[...]


def project(tiles, numbers, weights, before, final):
    arrays, tile_of = [], []
    for row in tiles:
        tile_of.append([])
        for array, start in row:
            known = [i for i, a in enumerate(arrays) if a is array]
            if not known:
                known = [len(arrays)]
                arrays.append(array)
            tile_of[-1].append((known[0], start))
    blocks = len(weights)
    widths = [w.shape[1] for w in weights[0]]
    depth = weights[0][0].shape[0]
    columns = sum(widths)
    tile_rows = tiles[0][1][1] + tiles[1][0][1]
    per_piece = arrays[0].shape[1] // depth
    here = lax.axis_index("tensor")
    where = []
    for number in numbers:
        where += [(number // per_piece) ^ here, number % per_piece * depth]
    where = jnp.stack(where).astype(jnp.int32)
    flat = [w for block in weights for w in block]
    operands = arrays + flat + ([] if before is None else [before])
    plan = (len(arrays), tile_of, blocks, widths, before is not None, final)
    slots = 3
    return pl.pallas_call(
        functools.partial(project_kernel, plan),
        grid_spec=pltpu.PrefetchScalarGridSpec(
            num_scalar_prefetch=1,
            grid=(1,),
            in_specs=[pl.BlockSpec(memory_space=pl.ANY)] * len(operands),
            out_specs=pl.BlockSpec((4, tile_rows, columns), lambda i, w: (0, 0, 0)),
            scratch_shapes=[
                pltpu.VMEM((slots, tile_rows, depth), bf16),
                pltpu.VMEM((blocks, depth, columns), bf16),
                pltpu.VMEM((4, tile_rows, columns), f32),
                pltpu.SemaphoreType.DMA((slots,)),
                pltpu.SemaphoreType.DMA((len(flat),)),
                pltpu.SemaphoreType.DMA,
            ],
        ),
        out_shape=jax.ShapeDtypeStruct((4, tile_rows, columns), bf16 if final else f32),
        compiler_params=pltpu.CompilerParams(vmem_limit_bytes=48 * 1024 * 1024),
        cost_estimate=pl.CostEstimate(
            flops=8 * tile_rows * depth * blocks * columns,
            bytes_accessed=8 * tile_rows * depth * blocks,
            transcendentals=0,
        ),
        name="project",
    )(where, *operands)


def reward_kernel(kg_ref, q_ref, old_key_ref, old_value_ref, key_ref, value_ref, grade_ref, so_far_ref, out_ref):
    span = q_ref.shape[0]
    context = old_key_ref.shape[1]
    rate = HD**-0.5 * math.log2(math.e)
    queries = q_ref[...]
    grade = grade_ref[0]
    block = math.gcd(512, context)
    peak = jnp.full((8, span), -jnp.inf, f32)
    total = jnp.zeros((8, span), f32)
    graded = jnp.zeros((8, span), f32)
    places = [(old_key_ref.at[0], old_value_ref.at[0], i, block) for i in range(0, context, block)]
    places.append((key_ref, value_ref, 0, span))
    for keys, values, start, size in places:
        scores = lax.dot_general(
            keys[start : start + size, :],
            queries,
            (((1,), (1,)), ((), ())),
            preferred_element_type=f32,
        )
        worth = jnp.dot(values[start : start + size, :], grade, preferred_element_type=f32)
        worth = worth[:, :HD] + worth[:, HD:]
        if keys is key_ref:
            shape = (size, span)
            visible = lax.broadcasted_iota(jnp.int32, shape, 0) <= lax.broadcasted_iota(
                jnp.int32, shape, 1
            )
            scores = jnp.where(visible, scores, masked_value)
        scores = scores.reshape(size // 8, 8, span)
        worth = worth.reshape(size // 8, 8, HD)
        new_peak = jnp.maximum(peak, jnp.max(scores, axis=0))
        fade = jnp.exp2((peak - new_peak) * rate)
        weights = jnp.exp2((scores - new_peak[None]) * rate)
        total = total * fade + jnp.sum(weights, axis=0)
        worth = jnp.concatenate([worth] * (span // HD), axis=2)
        graded = graded * fade + jnp.sum(weights * worth, axis=0)
        peak = new_peak
    top = jnp.max(peak, axis=0, keepdims=True)
    fade = jnp.exp2((peak - top) * rate)
    total = jnp.sum(total * fade, axis=0, keepdims=True)
    graded = jnp.sum(graded * fade, axis=0, keepdims=True)
    result = jnp.broadcast_to(graded / total, (8, span))

    @pl.when(pl.program_id(1) == 0)
    def _():
        out_ref[0] = so_far_ref[0] + result

    @pl.when(pl.program_id(1) != 0)
    def _():
        out_ref[0] += result


def grading_columns(grading):
    high = lax.reduce_precision(grading, 8, 7)
    parts = []
    for part in (high, grading - high):
        part = part.astype(bf16).reshape(-1, HD)
        parts.append(jnp.broadcast_to(part[:, :, None], (part.shape[0], HD, HD)))
    return jnp.concatenate(parts, axis=2)


def reward_share(queries, first_head, per_group, stored, fresh, grades, so_far):
    cands, context, _ = stored.shape
    span = queries.shape[0] // cands
    heads = queries.shape[1] // HD
    numbers = first_head + lax.broadcasted_iota(jnp.int32, (heads,), 0)
    groups = numbers // per_group
    grade = lax.dynamic_slice_in_dim(grades, first_head, heads, 0)
    spec = pltpu.PrefetchScalarGridSpec(
        num_scalar_prefetch=1,
        grid=(cands, heads),
        in_specs=[
            pl.BlockSpec((span, HD), lambda c, h, g: (c, h)),
            pl.BlockSpec((1, context, HD), lambda c, h, g: (c, 0, 2 * g[h])),
            pl.BlockSpec((1, context, HD), lambda c, h, g: (c, 0, 2 * g[h] + 1)),
            pl.BlockSpec((span, HD), lambda c, h, g: (c, 2 * g[h])),
            pl.BlockSpec((span, HD), lambda c, h, g: (c, 2 * g[h] + 1)),
            pl.BlockSpec((1, HD, 2 * HD), lambda c, h, g: (h, 0, 0)),
            pl.BlockSpec((1, 8, span), lambda c, h, g: (c, 0, 0)),
        ],
        out_specs=pl.BlockSpec((1, 8, span), lambda c, h, g: (c, 0, 0)),
    )
    cells = cands * heads * span * (context + span)
    return pl.pallas_call(
        reward_kernel,
        grid_spec=spec,
        out_shape=jax.ShapeDtypeStruct((cands, 8, span), f32),
        compiler_params=pltpu.CompilerParams(vmem_limit_bytes=40 * 1024 * 1024),
        cost_estimate=pl.CostEstimate(
            flops=6 * HD * cells, bytes_accessed=4 * stored.size, transcendentals=cells
        ),
        name="reward_share",
    )(groups, queries, stored, stored, fresh, fresh, grade, so_far)


def policy(stored, extents, kept, probes, pairs):
    cand_here = stored.shape[0]
    device_here = lax.axis_index("cand")
    devices = lax.axis_size("cand")
    key_scale = HD ** (-0.5)
    slots_here = probes.shape[0]
    lane_number = kept.shape[0]
    new_count = probes.shape[1]
    kv_here = stored.shape[2]
    policy_heads = probes.shape[2] // HD
    policy_group = policy_heads // kv_here
    cache_len = stored.shape[1]
    own = jnp.concatenate([probes, pairs], axis=2)
    everyone = jnp.zeros((lane_number,) + own.shape[1:], own.dtype)
    for step in range(devices):
        part = shifted(own, "cand", step) if step else own
        at = (device_here - step) % devices * slots_here
        everyone = lax.dynamic_update_slice(everyone, part, (at, 0, 0))
    causal_new = lax.broadcasted_iota(jnp.int32, (new_count, new_count), 0) >= lax.broadcasted_iota(
        jnp.int32, (new_count, new_count), 1
    )
    ids_here = device_here * cand_here + lax.broadcasted_iota(jnp.int32, (cand_here,), 0)
    matched = kept[None, :] == ids_here[:, None]
    slot_index = jnp.sum(
        jnp.where(matched, lax.broadcasted_iota(jnp.int32, (cand_here, lane_number), 1), 0), axis=1
    )
    chosen = jnp.take(everyone, slot_index, axis=0)
    own_queries = chosen[:, :, : policy_heads * HD].reshape(
        cand_here, new_count, kv_here, policy_group, HD
    )
    own_fresh = chosen[:, :, policy_heads * HD :].reshape(cand_here, new_count, kv_here, 2 * HD)
    living = lax.broadcasted_iota(jnp.int32, (cand_here, cache_len), 1)
    living = living < jnp.take(extents, ids_here)[:, None]
    living = living[:, None, None, None, :]
    scores = (
        jnp.einsum("cikgd,ctkd->ckgit", own_queries, stored[..., :HD], preferred_element_type=f32)
        * key_scale
    )
    scores = jnp.where(living, scores, masked_value)
    fresh_scores = (
        jnp.einsum("cikgd,cjkd->ckgij", own_queries, own_fresh[..., :HD], preferred_element_type=f32)
        * key_scale
    )
    fresh_scores = jnp.where(causal_new, fresh_scores, masked_value)
    peak_score = jnp.maximum(jnp.max(scores, axis=-1), jnp.max(fresh_scores, axis=-1))
    old_weights = jnp.where(living, jnp.exp(scores - peak_score[..., None]), 0.0)
    fresh_weights = jnp.where(causal_new, jnp.exp(fresh_scores - peak_score[..., None]), 0.0)
    denominator = jnp.sum(old_weights, axis=-1) + jnp.sum(fresh_weights, axis=-1)
    numerator = jnp.einsum(
        "ckgit,ctkd->ckgid", old_weights, stored[..., HD:], preferred_element_type=f32
    )
    numerator = numerator + jnp.einsum(
        "ckgij,cjkd->ckgid", fresh_weights, own_fresh[..., HD:], preferred_element_type=f32
    )
    result = numerator / denominator[..., None]
    flattened = jnp.transpose(result, (0, 3, 1, 2, 4)).reshape(
        cand_here, new_count * policy_heads * HD
    )
    placed = jnp.einsum(
        "cs,cx->sx", matched.astype(f32), flattened, precision=lax.Precision.HIGHEST
    )
    placed = placed.reshape(lane_number, new_count, policy_heads * HD).astype(bf16)
    rows = jnp.zeros((slots_here,) + placed.shape[1:], f32)
    for step in range(devices):
        at = (device_here + step) % devices * slots_here
        part = lax.dynamic_slice_in_dim(placed, at, slots_here, 0)
        rows = rows + (shifted(part, "cand", step) if step else part).astype(f32)
    return rows.astype(bf16)


def local(
    response_latest_embeddings,
    critic_probe_projector,
    critic_pair_projector,
    critic_stored_pairs,
    critic_grading_vector,
    actor_stored_pairs,
    filled_extents,
    kept_responses,
    actor_latest_probes,
    actor_latest_pairs,
):
    cand_here, span_len, _ = response_latest_embeddings.shape
    rows = cand_here * span_len
    devices = lax.axis_size("cand")
    group = lax.axis_index("groups")
    place = lax.axis_index("cand")
    depth, query_cols = critic_probe_projector.shape
    keyval_cols = critic_pair_projector.shape[1]
    heads_here = query_cols // HD
    per_group = heads_here // (keyval_cols // (2 * HD))
    query_half, keyval_half = query_cols // 2, keyval_cols // 2

    heads_half = heads_here // 2
    own_keyval = lax.dynamic_slice(
        critic_pair_projector, (0, group * keyval_half), (depth, keyval_half)
    )
    own_query = lax.dynamic_slice(
        critic_probe_projector, (0, group * query_half), (depth, query_half)
    )
    chunks = [own_keyval] + [own_query[:, h * HD : (h + 1) * HD] for h in range(heads_half)]
    rings = [chunks]
    tiles = gather_rows(response_latest_embeddings, rows)
    last = devices - 1
    for step in range(last - 1):
        rings.append([shifted(w, "cand", 1) for w in rings[-1]])
    numbers = [(place - step) % devices for step in range(devices)]
    early = project(tiles, numbers[:2], rings[:2], None, False)
    sums = project(tiles, numbers[2:last], rings[2:last], early, False) if last > 2 else early
    waiting = list(rings[-1])
    waiting[-1] = after(waiting[-1], sums)
    rings.append([shifted(w, "cand", 1) for w in waiting])

    grades = grading_columns(critic_grading_vector)
    starts = [0]
    for w in chunks:
        starts.append(starts[-1] + w.shape[1])

    def finish(index, *earlier):
        weights = rings[last][index]
        if earlier:
            weights = after(weights, *earlier)
        before = sums[:, :, starts[index] : starts[index + 1]]
        done = project(tiles, numbers[last:], [[weights]], before, True)
        mine = done[:2].reshape(rows, -1)
        return mine, partner(done[2:].reshape(rows, -1), "groups", 1)

    kept, sent = finish(0)
    keyval = jnp.where(
        group == 0,
        jnp.concatenate([kept, sent], axis=1),
        jnp.concatenate([sent, kept], axis=1),
    )
    share = jnp.zeros((cand_here, 8, span_len), f32)

    def score(queries, owner, head, share):
        return reward_share(
            queries, owner * heads_half + head, per_group, critic_stored_pairs, keyval, grades, share
        )

    kept, sent = finish(1)
    for head in range(heads_half):
        share = score(kept, group, head, share)
        if head + 1 < heads_half:
            kept, next_sent = finish(head + 2, share)
            sent = after(sent, kept)
        share = score(sent, 1 - group, head, share)
        sent = next_sent
    share = share[:, 0, :]
    tensor = lax.axis_size("tensor")
    terms = [share] + [partner(share, "tensor", bits) for bits in range(1, tensor)]
    while len(terms) > 1:
        terms = [a + b for a, b in zip(terms[::2], terms[1::2])]
    slot_rows = policy(
        actor_stored_pairs, filled_extents, kept_responses, actor_latest_probes, actor_latest_pairs
    )
    return terms[0], slot_rows


def solution(mesh):
    placed = (
        P(("groups", "cand"), None, "tensor"),
        P("cand", "tensor"),
        P("cand", "tensor"),
        P(("groups", "cand"), None, "tensor"),
        P("tensor"),
        P(("groups", "cand"), None, "tensor", None),
        P("groups"),
        P("groups"),
        P(("groups", "cand"), None, "tensor"),
        P(("groups", "cand"), None, "tensor"),
    )
    return jax.shard_map(
        local,
        mesh=mesh,
        in_specs=placed,
        out_specs=(P(("groups", "cand"), None), P(("groups", "cand"), None, "tensor")),
        check_vma=False,
    )
```

```python
import functools
import math

import jax
import jax.numpy as jnp
from jax import lax
from jax.experimental import pallas as pl
from jax.experimental.pallas import tpu as pltpu
from jax.sharding import PartitionSpec as P

HD = 128
masked_value = -1e30
bf16, f32 = jnp.bfloat16, jnp.float32


def touch(arrays):
    anywhere = pl.BlockSpec(memory_space=pl.ANY)
    return pl.pallas_call(
        lambda *refs: None,
        in_specs=[anywhere] * len(arrays),
        out_specs=[anywhere] * len(arrays),
        out_shape=[jax.ShapeDtypeStruct(v.shape, v.dtype) for v in arrays],
        input_output_aliases={i: i for i in range(len(arrays))},
        compiler_params=pltpu.CompilerParams(vmem_limit_bytes=60 * 1024 * 1024),
        cost_estimate=pl.CostEstimate(flops=0, bytes_accessed=0, transcendentals=0),
        name="touch",
    )(*arrays)


def shifted(value, axis, step):
    size = lax.axis_size(axis)
    return lax.ppermute(value, axis, [(i, (i + step) % size) for i in range(size)])


def partner(value, axis, bits):
    size = lax.axis_size(axis)
    return lax.ppermute(value, axis, [(i, i ^ bits) for i in range(size)])


def project_kernel(plan, where_ref, *refs):
    sources, cands, blocks, widths, begin, has_sum = plan
    arrays, refs = refs[:sources], refs[sources:]
    weights, refs = refs[: blocks * len(widths)], refs[blocks * len(widths) :]
    before, refs = (refs[0], refs[1:]) if has_sum else (None, refs)
    out, tile_buf, weight_buf, sum_buf, tile_sem, weight_sem, sum_sem = refs
    slots, tile_rows, depth = tile_buf.shape
    columns = sum_buf.shape[2]
    steps = cands * blocks

    def load(item):
        block, tile = item // cands, item % cands
        off, column = where_ref[2 * block], where_ref[2 * block + 1]
        column = pl.multiple_of(column, depth)
        slot = lax.rem(item, slots)
        for i in range(sources):

            @pl.when(off == i)
            def _():
                pltpu.make_async_copy(
                    arrays[i].at[tile, :, pl.ds(column, depth)], tile_buf.at[slot], tile_sem.at[slot]
                ).start()

    copies = []
    for block in range(blocks):
        at = 0
        for j, width in enumerate(widths):
            number = block * len(widths) + j
            copies.append(
                pltpu.make_async_copy(
                    weights[number].at[0:depth, :],
                    weight_buf.at[block, :, at : at + width],
                    weight_sem.at[number],
                )
            )
            at += width
    first = len(widths)
    for copy in copies[:first]:
        copy.start()
    for item in range(min(slots - 1, steps)):
        load(item)
    if has_sum:
        columns_of = before.at[:, :, begin : begin + columns]
        copies.append(pltpu.make_async_copy(columns_of, sum_buf, sum_sem))
    for copy in copies[first:]:
        copy.start()
    for copy in copies:
        copy.wait()

    def step(item, _):
        @pl.when(item + slots - 1 < steps)
        def _():
            load(item + slots - 1)

        slot = lax.rem(item, slots)
        block, tile = item // cands, item % cands
        pltpu.make_async_copy(
            arrays[0].at[0, :, pl.ds(0, depth)], tile_buf.at[slot], tile_sem.at[slot]
        ).wait()
        term = jnp.dot(tile_buf[slot], weight_buf[block], preferred_element_type=f32)
        if has_sum:
            term = term + sum_buf[tile]
        else:
            term = jnp.where(block > 0, term + sum_buf[tile], term)
        if blocks > 1:
            sum_buf[tile] = term

        @pl.when(block == blocks - 1)
        def _():
            out[tile] = term.astype(out.dtype)

        return 0

    lax.fori_loop(0, steps, step, 0)


def project(pieces, numbers, depth, weights, before, begin, final):
    here = lax.axis_index("tensor")
    cands, tile_rows, width = pieces[0].shape
    blocks = len(weights)
    widths = [w.shape[1] for w in weights[0]]
    columns = sum(widths)
    per_piece = width // depth
    where = []
    for number in numbers:
        where += [(number // per_piece) ^ here, number % per_piece * depth]
    where = jnp.stack(where).astype(jnp.int32)
    flat = [w for block in weights for w in block]
    operands = list(pieces) + flat + ([] if before is None else [before])
    plan = (len(pieces), cands, blocks, widths, begin, before is not None)
    slots = 3
    return pl.pallas_call(
        functools.partial(project_kernel, plan),
        in_specs=[pl.BlockSpec(memory_space=pltpu.SMEM)]
        + [pl.BlockSpec(memory_space=pl.ANY)] * len(operands),
        out_specs=pl.BlockSpec(memory_space=pltpu.VMEM),
        out_shape=jax.ShapeDtypeStruct((cands, tile_rows, columns), bf16 if final else f32),
        scratch_shapes=[
            pltpu.VMEM((slots, tile_rows, depth), bf16),
            pltpu.VMEM((blocks, depth, columns), bf16),
            pltpu.VMEM((cands, tile_rows, columns), f32),
            pltpu.SemaphoreType.DMA((slots,)),
            pltpu.SemaphoreType.DMA((len(flat),)),
            pltpu.SemaphoreType.DMA,
        ],
        compiler_params=pltpu.CompilerParams(vmem_limit_bytes=60 * 1024 * 1024),
        cost_estimate=pl.CostEstimate(
            flops=2 * cands * tile_rows * depth * blocks * columns,
            bytes_accessed=2 * cands * tile_rows * depth * blocks,
            transcendentals=0,
        ),
        name="project",
    )(where, *operands)


def reward_kernel(kg_ref, q_ref, old_key_ref, old_value_ref, key_ref, value_ref, grade_ref, so_far_ref, out_ref):
    span = q_ref.shape[0]
    context = old_key_ref.shape[1]
    rate = HD**-0.5 * math.log2(math.e)
    queries = q_ref[...]
    grade = grade_ref[0]
    block = math.gcd(HD, context)
    peak = jnp.full((8, span), -jnp.inf, f32)
    total = jnp.zeros((8, span), f32)
    graded = jnp.zeros((8, span), f32)
    places = [(old_key_ref.at[0], old_value_ref.at[0], i) for i in range(0, context, block)]
    places += [(key_ref, value_ref, i) for i in range(0, span, block)]

    def products(keys, values, start):
        scores = lax.dot_general(
            keys[start : start + block, :],
            queries,
            (((1,), (1,)), ((), ())),
            preferred_element_type=f32,
        )
        worth = jnp.dot(values[start : start + block, :], grade, preferred_element_type=f32)
        worth = worth[:, :HD] + worth[:, HD:]
        if keys is key_ref:
            shape = (block, span)
            visible = start + lax.broadcasted_iota(jnp.int32, shape, 0) <= (
                lax.broadcasted_iota(jnp.int32, shape, 1)
            )
            scores = jnp.where(visible, scores, masked_value)
        return scores.reshape(block // 8, 8, span), worth.reshape(block // 8, 8, HD)

    coming = products(*places[0])
    for number in range(len(places)):
        scores, worth = coming
        if number + 1 < len(places):
            coming = products(*places[number + 1])
        new_peak = jnp.maximum(peak, jnp.max(scores, axis=0))
        fade = jnp.exp2((peak - new_peak) * rate)
        weights = jnp.exp2((scores - new_peak[None]) * rate)
        total = total * fade + jnp.sum(weights, axis=0)
        worth = jnp.concatenate([worth] * (span // HD), axis=2)
        graded = graded * fade + jnp.sum(weights * worth, axis=0)
        peak = new_peak
    top = jnp.max(peak, axis=0, keepdims=True)
    fade = jnp.exp2((peak - top) * rate)
    total = jnp.sum(total * fade, axis=0, keepdims=True)
    graded = jnp.sum(graded * fade, axis=0, keepdims=True)
    result = jnp.broadcast_to(graded / total, (8, span))

    @pl.when(pl.program_id(1) == 0)
    def _():
        out_ref[0] = so_far_ref[0] + result

    @pl.when(pl.program_id(1) != 0)
    def _():
        out_ref[0] += result


def grading_columns(grading):
    high = lax.reduce_precision(grading, 8, 7)
    parts = []
    for part in (high, grading - high):
        part = part.astype(bf16).reshape(-1, HD)
        parts.append(jnp.broadcast_to(part[:, :, None], (part.shape[0], HD, HD)))
    return jnp.concatenate(parts, axis=2)


def reward_share(queries, first_block, numbers, stored, per_group, fresh, fresh_block, grades, so_far):
    cands, context, _ = stored.shape
    span = queries.shape[0] // cands
    heads = len(numbers)
    scalars = []
    for number in numbers:
        pair = number // per_group
        scalars += [number, 2 * pair, fresh_block(2 * pair), fresh_block(2 * pair + 1)]
    scalars = jnp.stack(scalars).astype(jnp.int32)
    spec = pltpu.PrefetchScalarGridSpec(
        num_scalar_prefetch=1,
        grid=(cands, heads),
        in_specs=[
            pl.BlockSpec((span, HD), lambda c, h, n: (c, first_block + h)),
            pl.BlockSpec((1, context, HD), lambda c, h, n: (c, 0, n[4 * h + 1])),
            pl.BlockSpec((1, context, HD), lambda c, h, n: (c, 0, n[4 * h + 1] + 1)),
            pl.BlockSpec((span, HD), lambda c, h, n: (c, n[4 * h + 2])),
            pl.BlockSpec((span, HD), lambda c, h, n: (c, n[4 * h + 3])),
            pl.BlockSpec((1, HD, 2 * HD), lambda c, h, n: (n[4 * h], 0, 0)),
            pl.BlockSpec((1, 8, span), lambda c, h, n: (c, 0, 0)),
        ],
        out_specs=pl.BlockSpec((1, 8, span), lambda c, h, n: (c, 0, 0)),
    )
    cells = cands * heads * span * (context + span)
    return pl.pallas_call(
        reward_kernel,
        grid_spec=spec,
        out_shape=jax.ShapeDtypeStruct((cands, 8, span), f32),
        compiler_params=pltpu.CompilerParams(vmem_limit_bytes=60 * 1024 * 1024),
        cost_estimate=pl.CostEstimate(
            flops=6 * HD * cells, bytes_accessed=4 * stored.size, transcendentals=cells
        ),
        name="reward_share",
    )(scalars, queries, stored, stored, fresh, fresh, grades, so_far)


def send_slots(placed, slots_here):
    devices = lax.axis_size("cand")
    here = lax.axis_index("cand")
    bit = devices // 2
    while bit:
        half = bit * slots_here
        low = (here & bit) == 0
        first, second = placed[:half], placed[half:]
        new = partner(jnp.where(low, second, first), "cand", bit)
        placed = jnp.where(low, first, second) + new
        bit //= 2
    return placed


def policy_rows(stored, extents, kept, everyone):
    cand_here = stored.shape[0]
    device_here = lax.axis_index("cand")
    key_scale = HD ** (-0.5)
    lane_number = kept.shape[0]
    new_count = everyone.shape[1]
    kv_here = stored.shape[2]
    policy_heads = everyone.shape[2] // HD - 2 * kv_here
    policy_group = policy_heads // kv_here
    cache_len = stored.shape[1]
    causal_new = lax.broadcasted_iota(jnp.int32, (new_count, new_count), 0) >= lax.broadcasted_iota(
        jnp.int32, (new_count, new_count), 1
    )
    ids_here = device_here * cand_here + lax.broadcasted_iota(jnp.int32, (cand_here,), 0)
    matched = kept[None, :] == ids_here[:, None]
    slot_index = jnp.sum(
        jnp.where(matched, lax.broadcasted_iota(jnp.int32, (cand_here, lane_number), 1), 0), axis=1
    )
    chosen = jnp.take(everyone, slot_index, axis=0)
    own_queries = chosen[:, :, : policy_heads * HD].reshape(
        cand_here, new_count, kv_here, policy_group, HD
    )
    own_fresh = chosen[:, :, policy_heads * HD :].reshape(cand_here, new_count, kv_here, 2 * HD)
    living = lax.broadcasted_iota(jnp.int32, (cand_here, cache_len), 1)
    living = living < jnp.take(extents, ids_here)[:, None]
    living = living[:, None, None, None, :]
    scores = (
        jnp.einsum("cikgd,ctkd->ckgit", own_queries, stored[..., :HD], preferred_element_type=f32)
        * key_scale
    )
    scores = jnp.where(living, scores, masked_value)
    fresh_scores = (
        jnp.einsum("cikgd,cjkd->ckgij", own_queries, own_fresh[..., :HD], preferred_element_type=f32)
        * key_scale
    )
    fresh_scores = jnp.where(causal_new, fresh_scores, masked_value)
    peak_score = jnp.maximum(jnp.max(scores, axis=-1), jnp.max(fresh_scores, axis=-1))
    old_weights = jnp.where(living, jnp.exp(scores - peak_score[..., None]), 0.0)
    fresh_weights = jnp.where(causal_new, jnp.exp(fresh_scores - peak_score[..., None]), 0.0)
    denominator = jnp.sum(old_weights, axis=-1) + jnp.sum(fresh_weights, axis=-1)
    numerator = jnp.einsum(
        "ckgit,ctkd->ckgid", old_weights, stored[..., HD:], preferred_element_type=f32
    )
    numerator = numerator + jnp.einsum(
        "ckgij,cjkd->ckgid", fresh_weights, own_fresh[..., HD:], preferred_element_type=f32
    )
    result = numerator / denominator[..., None]
    flattened = jnp.transpose(result, (0, 3, 1, 2, 4)).reshape(
        cand_here, new_count * policy_heads * HD
    )
    placed = jnp.einsum(
        "cs,cx->sx", matched.astype(f32), flattened, precision=lax.Precision.HIGHEST
    )
    return placed.reshape(lane_number, new_count, policy_heads * HD).astype(bf16)


def local(
    response_latest_embeddings,
    critic_probe_projector,
    critic_pair_projector,
    critic_stored_pairs,
    critic_grading_vector,
    actor_stored_pairs,
    filled_extents,
    kept_responses,
    actor_latest_probes,
    actor_latest_pairs,
):
    cand_here, span_len, _ = response_latest_embeddings.shape
    rows = cand_here * span_len
    devices = lax.axis_size("cand")
    group = lax.axis_index("groups")
    place = lax.axis_index("cand")
    depth, query_cols = critic_probe_projector.shape
    keyval_cols = critic_pair_projector.shape[1]
    heads_here = query_cols // HD
    per_group = heads_here // (keyval_cols // (2 * HD))
    query_half, keyval_half = query_cols // 2, keyval_cols // 2

    heads_half = heads_here // 2
    last = devices - 1
    tensor = lax.axis_size("tensor")

    def half_of(owner):
        pair = lax.dynamic_slice(critic_pair_projector, (0, owner * keyval_half), (depth, keyval_half))
        probe = lax.dynamic_slice(
            critic_probe_projector, (0, owner * query_half), (depth, query_half)
        )
        both = [pair[:, i : i + HD] for i in range(0, keyval_half, HD)]
        return both + [probe[:, i : i + HD] for i in range(0, query_half, HD)]

    mine, theirs = half_of(group), half_of(1 - group)
    count = len(mine)
    pairs = count - heads_half
    slots = jnp.concatenate([actor_latest_probes, actor_latest_pairs], axis=2)
    extra = slots.size // HD
    padding = -extra % 16
    mine[0] = jnp.concatenate([mine[0], slots.reshape(extra, HD), jnp.zeros((padding, HD), bf16)])
    value = {("w", 0, i): w for i, w in enumerate(mine)}
    value.update({("v", 0, i): w for i, w in enumerate(theirs)})

    value["token"] = jnp.zeros((8, HD), f32)

    def gate(*names):
        names = ["token"] + list(names)
        for name, array in zip(names, touch([value[n] for n in names])):
            value[name] = array

    value["own", 0] = response_latest_embeddings
    bits = [1 << b for b in range(int(math.log2(tensor)) - 1, -1, -1)]
    held = [0]
    for bit in bits[:-1]:
        for off in list(held):
            value["own", off ^ bit] = partner(value["own", off], "tensor", bit)
            held.append(off ^ bit)
    value["own", 1] = partner(value["own", 0], "tensor", 1)

    wide = 2
    groups = [range(low, min(pairs, low + wide)) for low in range(0, pairs, wide)]
    groups += [range(low, min(count, low + wide)) for low in range(pairs, count, wide)]
    hops = [(step, i) for chosen in groups for step in range(last) for i in chosen]
    total = len(hops)
    extras = {}

    def at(number, *names):
        extras.setdefault(min(number, total + wide - 1), []).extend(names)

    def arrived(number):
        step, i = hops[number]
        return step + 1, i

    numbers = [(place - step) % devices for step in range(devices)]

    def multiply(begin, end, names, before, column, final):
        weights = [[value[side, step, i] for side, i in names] for step in range(begin, end)]
        pieces = [value["own", off] for off in range(tensor)]
        done = project(pieces, numbers[begin:end], depth, weights, before, column, final)
        return done.reshape(rows, -1) if final else done

    grades = grading_columns(critic_grading_vector)
    value["share"] = jnp.zeros((cand_here, 8, span_len), f32)
    near = [off for off in held if off]
    def cross():
        for off in near:
            value["own", off ^ 1] = partner(value["own", off], "tensor", 1)
        at(now + 1, *[("own", off ^ 1) for off in near])

    def policy_now():
        everyone = jnp.zeros((devices * slots.shape[0],) + slots.shape[1:], bf16)
        for step in range(devices):
            part = value["w", step, 0][depth : depth + extra].reshape(slots.shape)
            start = (place - step) % devices * slots.shape[0]
            everyone = lax.dynamic_update_slice(everyone, part, (start, 0, 0))
        value["policy"] = policy_rows(
            actor_stored_pairs, filled_extents, kept_responses, everyone
        )
        at(now + 3, "policy")

    def fresh_block(chunk):
        return jnp.where(chunk // pairs == group, 0, pairs) + chunk % pairs

    def score(queries, first_block, heads):
        owners = {"w": group, "v": 1 - group}
        numbers = [owners[side] * heads_half + i - pairs for side, i in heads]
        value["share"] = reward_share(
            queries,
            first_block,
            numbers,
            critic_stored_pairs,
            per_group,
            value["initial"],
            fresh_block,
            grades,
            value["share"],
        )

    def keyval_now():
        names = [(side, i) for side in "wv" for i in range(pairs)]
        value["initial"] = multiply(0, devices, names, None, 0, True)
        at(now + 2, "initial")

    def both(chosen):
        return [(side, i) for i in chosen for side in "wv"]

    def some_now(chosen, first, end):
        before = value.get(("sums", chosen))
        value["sums", chosen] = multiply(first, end, both(chosen), before, 0, False)
        at(now + 2, ("sums", chosen))

    def scores_now(chosen, part):
        column = 2 * HD * chosen.index(part[0])
        heads = both(part)
        value["queries"] = multiply(last, devices, heads, value["sums", chosen], column, True)
        score(value["queries"], 0, heads)
        at(now + 3, "share")

    lag = 2

    def seen_at(step, i):
        return hops.index((step, i)) + wide + lag

    acts = [(seen_at(last - 1, 0) - lag, policy_now)]
    acts.append((seen_at(last - 1, pairs - 1), keyval_now))
    for chosen in groups:
        if chosen[0] < pairs:
            continue
        end = chosen[-1]
        if chosen is groups[-1]:
            acts.append((seen_at(0, end), functools.partial(some_now, chosen, 0, 2)))
            if last > 2:
                acts.append((seen_at(last - 2, end), functools.partial(some_now, chosen, 2, last)))
        else:
            acts.append((seen_at(last - 2, end), functools.partial(some_now, chosen, 0, last)))
            acts.append((seen_at(last - 1, end), functools.partial(scores_now, chosen, chosen)))
    acts.append((min(8, total // 2), cross))
    at(total + wide - 1, "policy")
    at(wide, ("own", 1))
    at(min(8, total // 2), *[("own", off) for off in near])
    for now in range(total + wide + lag):
        names = []
        if 0 <= now - wide < total:
            names.append(("w",) + arrived(now - wide))
        if 0 <= now - wide - lag < total:
            names.append(("v",) + arrived(now - wide - lag))
        if now < total and hops[now][0] == 0 and now >= wide:
            names.append(("w",) + hops[now])
        names += extras.pop(now, [])
        if now >= wide:
            gate(*names)
        if now < total:
            step, i = hops[now]
            value["w", step + 1, i] = shifted(value["w", step, i], "cand", 1)
        if 0 <= now - wide < total:
            step, i = arrived(now - wide)
            value["v", step, i] = partner(value["w", step, i], "groups", 1)
        for when, act in acts:
            if when == now:
                act()

    chosen = groups[-1]
    for i in chosen:
        if i != chosen[0]:
            gate(("w", last, i), ("v", last, i), "share")
        scores_now(chosen, [i])
    slot_rows = send_slots(value["policy"], slots.shape[0])
    share = value["share"]
    share = share[:, 0, :]
    terms = [share] + [partner(share, "tensor", bits) for bits in range(1, tensor)]
    while len(terms) > 1:
        terms = [a + b for a, b in zip(terms[::2], terms[1::2])]
    return terms[0], slot_rows


def solution(mesh):
    placed = (
        P(("groups", "cand"), None, "tensor"),
        P("cand", "tensor"),
        P("cand", "tensor"),
        P(("groups", "cand"), None, "tensor"),
        P("tensor"),
        P(("groups", "cand"), None, "tensor", None),
        P("groups"),
        P("groups"),
        P(("groups", "cand"), None, "tensor"),
        P(("groups", "cand"), None, "tensor"),
    )
    return jax.shard_map(
        local,
        mesh=mesh,
        in_specs=placed,
        out_specs=(P(("groups", "cand"), None), P(("groups", "cand"), None, "tensor")),
        check_vma=False,
    )
```

```python
import functools
import math

import jax
import jax.numpy as jnp
from jax import lax
from jax.experimental import pallas as pl
from jax.experimental.pallas import tpu as pltpu
from jax.sharding import PartitionSpec as P

HD = 128
masked_value = -1e30
bf16, f32 = jnp.bfloat16, jnp.float32


def touch(arrays):
    anywhere = pl.BlockSpec(memory_space=pl.ANY)
    return pl.pallas_call(
        lambda *refs: None,
        in_specs=[anywhere] * len(arrays),
        out_specs=[anywhere] * len(arrays),
        out_shape=[jax.ShapeDtypeStruct(v.shape, v.dtype) for v in arrays],
        input_output_aliases={i: i for i in range(len(arrays))},
        compiler_params=pltpu.CompilerParams(vmem_limit_bytes=60 * 1024 * 1024),
        cost_estimate=pl.CostEstimate(flops=0, bytes_accessed=0, transcendentals=0),
        name="touch",
    )(*arrays)


def shifted(value, axis, step):
    size = lax.axis_size(axis)
    return lax.ppermute(value, axis, [(i, (i + step) % size) for i in range(size)])


def partner(value, axis, bits):
    size = lax.axis_size(axis)
    return lax.ppermute(value, axis, [(i, i ^ bits) for i in range(size)])


def project_kernel(plan, where_ref, *refs):
    sources, tile_of, blocks, widths, begin, has_sum = plan
    arrays, refs = refs[:sources], refs[sources:]
    cands = len(tile_of[0])
    weights, refs = refs[: blocks * len(widths)], refs[blocks * len(widths) :]
    before, refs = (refs[0], refs[1:]) if has_sum else (None, refs)
    out, tile_buf, weight_buf, sum_buf, tile_sem, weight_sem, sum_sem = refs
    slots, tile_rows, depth = tile_buf.shape
    columns = sum_buf.shape[2]
    steps = cands * blocks

    def load(item):
        block, tile = item // cands, item % cands
        off, column = where_ref[2 * block], where_ref[2 * block + 1]
        column = pl.multiple_of(column, depth)
        slot = lax.rem(item, slots)
        for i, row in enumerate(tile_of):
            for j, (number, place) in enumerate(row):

                @pl.when((off == i) & (tile == j))
                def _():
                    whole = arrays[number] if place is None else arrays[number].at[place]
                    pltpu.make_async_copy(
                        whole.at[:, pl.ds(column, depth)], tile_buf.at[slot], tile_sem.at[slot]
                    ).start()

    copies = []
    for block in range(blocks):
        at = 0
        copies.append([])
        for j, width in enumerate(widths):
            number = block * len(widths) + j
            copies[-1].append(
                pltpu.make_async_copy(
                    weights[number].at[0:depth, :],
                    weight_buf.at[block, :, at : at + width],
                    weight_sem.at[number],
                )
            )
            at += width
    for copy in copies[0]:
        copy.start()
    for item in range(min(slots - 1, steps)):
        load(item)
    if has_sum:
        columns_of = before.at[:, :, begin : begin + columns]
        sum_copy = pltpu.make_async_copy(columns_of, sum_buf, sum_sem)
        sum_copy.start()
    for block in copies[1:]:
        for copy in block:
            copy.start()

    def step(item, _):
        @pl.when(item + slots - 1 < steps)
        def _():
            load(item + slots - 1)

        slot = lax.rem(item, slots)
        block, tile = item // cands, item % cands
        for i in range(blocks):

            @pl.when(item == i * cands)
            def _():
                for copy in copies[i]:
                    copy.wait()

        if has_sum:

            @pl.when(item == 0)
            def _():
                sum_copy.wait()

        pltpu.make_async_copy(
            arrays[0].at[0, :, pl.ds(0, depth)] if tile_of[0][0][1] is not None else arrays[0].at[:, pl.ds(0, depth)],
            tile_buf.at[slot],
            tile_sem.at[slot],
        ).wait()
        term = jnp.dot(tile_buf[slot], weight_buf[block], preferred_element_type=f32)
        if has_sum:
            term = term + sum_buf[tile]
        else:
            term = jnp.where(block > 0, term + sum_buf[tile], term)
        if blocks > 1:
            sum_buf[tile] = term

        @pl.when(block == blocks - 1)
        def _():
            out[tile] = term.astype(out.dtype)

        return 0

    lax.fori_loop(0, steps, step, 0)


def project(pieces, numbers, depth, weights, before, begin, final):
    here = lax.axis_index("tensor")
    cands, tile_rows, width = pieces[0].shape
    arrays, tile_of = [], []
    for piece in pieces:
        if isinstance(piece, list):
            tile_of.append([(len(arrays) + c, None) for c in range(cands)])
            arrays += piece
        else:
            tile_of.append([(len(arrays), c) for c in range(cands)])
            arrays.append(piece)
    blocks = len(weights)
    widths = [w.shape[1] for w in weights[0]]
    columns = sum(widths)
    per_piece = width // depth
    where = []
    for number in numbers:
        where += [(number // per_piece) ^ here, number % per_piece * depth]
    where = jnp.stack(where).astype(jnp.int32)
    flat = [w for block in weights for w in block]
    operands = arrays + flat + ([] if before is None else [before])
    plan = (len(arrays), tile_of, blocks, widths, begin, before is not None)
    slots = 3
    return pl.pallas_call(
        functools.partial(project_kernel, plan),
        in_specs=[pl.BlockSpec(memory_space=pltpu.SMEM)]
        + [pl.BlockSpec(memory_space=pl.ANY)] * len(operands),
        out_specs=pl.BlockSpec(memory_space=pltpu.VMEM),
        out_shape=jax.ShapeDtypeStruct((cands, tile_rows, columns), bf16 if final else f32),
        scratch_shapes=[
            pltpu.VMEM((slots, tile_rows, depth), bf16),
            pltpu.VMEM((blocks, depth, columns), bf16),
            pltpu.VMEM((cands, tile_rows, columns), f32),
            pltpu.SemaphoreType.DMA((slots,)),
            pltpu.SemaphoreType.DMA((len(flat),)),
            pltpu.SemaphoreType.DMA,
        ],
        compiler_params=pltpu.CompilerParams(vmem_limit_bytes=60 * 1024 * 1024),
        cost_estimate=pl.CostEstimate(
            flops=2 * cands * tile_rows * depth * blocks * columns,
            bytes_accessed=2 * cands * tile_rows * depth * blocks,
            transcendentals=0,
        ),
        name="project",
    )(where, *operands)


def reward_kernel(kg_ref, q_ref, old_key_ref, old_value_ref, key_ref, value_ref, grade_ref, so_far_ref, out_ref):
    span = q_ref.shape[0]
    context = old_key_ref.shape[1]
    rate = HD**-0.5 * math.log2(math.e)
    queries = q_ref[...]
    grade = grade_ref[0]
    block = math.gcd(HD, context)
    peak = jnp.full((8, span), -jnp.inf, f32)
    total = jnp.zeros((8, span), f32)
    graded = jnp.zeros((8, span), f32)
    places = [(old_key_ref.at[0], old_value_ref.at[0], i) for i in range(0, context, block)]
    places += [(key_ref, value_ref, i) for i in range(0, span, block)]

    def products(keys, values, start):
        scores = lax.dot_general(
            keys[start : start + block, :],
            queries,
            (((1,), (1,)), ((), ())),
            preferred_element_type=f32,
        )
        worth = jnp.dot(values[start : start + block, :], grade, preferred_element_type=f32)
        worth = worth[:, :HD] + worth[:, HD:]
        if keys is key_ref:
            shape = (block, span)
            visible = start + lax.broadcasted_iota(jnp.int32, shape, 0) <= (
                lax.broadcasted_iota(jnp.int32, shape, 1)
            )
            scores = jnp.where(visible, scores, masked_value)
        return scores.reshape(block // 8, 8, span), worth.reshape(block // 8, 8, HD)

    coming = products(*places[0])
    for number in range(len(places)):
        scores, worth = coming
        if number + 1 < len(places):
            coming = products(*places[number + 1])
        new_peak = jnp.maximum(peak, jnp.max(scores, axis=0))
        fade = jnp.exp2((peak - new_peak) * rate)
        weights = jnp.exp2((scores - new_peak[None]) * rate)
        total = total * fade + jnp.sum(weights, axis=0)
        worth = jnp.concatenate([worth] * (span // HD), axis=2)
        graded = graded * fade + jnp.sum(weights * worth, axis=0)
        peak = new_peak
    top = jnp.max(peak, axis=0, keepdims=True)
    fade = jnp.exp2((peak - top) * rate)
    total = jnp.sum(total * fade, axis=0, keepdims=True)
    graded = jnp.sum(graded * fade, axis=0, keepdims=True)
    result = jnp.broadcast_to(graded / total, (8, span))

    @pl.when(pl.program_id(1) == 0)
    def _():
        out_ref[0] = so_far_ref[0] + result

    @pl.when(pl.program_id(1) != 0)
    def _():
        out_ref[0] += result


def grading_columns(grading):
    high = lax.reduce_precision(grading, 8, 7)
    parts = []
    for part in (high, grading - high):
        part = part.astype(bf16).reshape(-1, HD)
        parts.append(jnp.broadcast_to(part[:, :, None], (part.shape[0], HD, HD)))
    return jnp.concatenate(parts, axis=2)


def reward_share(queries, first_block, numbers, stored, per_group, fresh, fresh_block, grades, so_far):
    cands, context, _ = stored.shape
    span = queries.shape[0] // cands
    heads = len(numbers)
    scalars = []
    for number in numbers:
        pair = number // per_group
        scalars += [number, 2 * pair, fresh_block(2 * pair), fresh_block(2 * pair + 1)]
    scalars = jnp.stack(scalars).astype(jnp.int32)
    spec = pltpu.PrefetchScalarGridSpec(
        num_scalar_prefetch=1,
        grid=(cands, heads),
        in_specs=[
            pl.BlockSpec((span, HD), lambda c, h, n: (c, first_block + h)),
            pl.BlockSpec((1, context, HD), lambda c, h, n: (c, 0, n[4 * h + 1])),
            pl.BlockSpec((1, context, HD), lambda c, h, n: (c, 0, n[4 * h + 1] + 1)),
            pl.BlockSpec((span, HD), lambda c, h, n: (c, n[4 * h + 2])),
            pl.BlockSpec((span, HD), lambda c, h, n: (c, n[4 * h + 3])),
            pl.BlockSpec((1, HD, 2 * HD), lambda c, h, n: (n[4 * h], 0, 0)),
            pl.BlockSpec((1, 8, span), lambda c, h, n: (c, 0, 0)),
        ],
        out_specs=pl.BlockSpec((1, 8, span), lambda c, h, n: (c, 0, 0)),
    )
    cells = cands * heads * span * (context + span)
    return pl.pallas_call(
        reward_kernel,
        grid_spec=spec,
        out_shape=jax.ShapeDtypeStruct((cands, 8, span), f32),
        compiler_params=pltpu.CompilerParams(vmem_limit_bytes=60 * 1024 * 1024),
        cost_estimate=pl.CostEstimate(
            flops=6 * HD * cells, bytes_accessed=4 * stored.size, transcendentals=cells
        ),
        name="reward_share",
    )(scalars, queries, stored, stored, fresh, fresh, grades, so_far)


def send_half(placed, slots_here, bit):
    low = (lax.axis_index("cand") & bit) == 0
    first, second = placed[: bit * slots_here], placed[bit * slots_here :]
    new = partner(jnp.where(low, second, first), "cand", bit)
    return jnp.where(low, first, second) + new


def policy_rows(stored, stored_values, extents, kept, everyone):
    cand_here = stored.shape[0]
    device_here = lax.axis_index("cand")
    key_scale = HD ** (-0.5)
    lane_number = kept.shape[0]
    new_count = everyone.shape[1]
    kv_here = stored.shape[2]
    policy_heads = everyone.shape[2] // HD - 2 * kv_here
    policy_group = policy_heads // kv_here
    cache_len = stored.shape[1]
    causal_new = lax.broadcasted_iota(jnp.int32, (new_count, new_count), 0) >= lax.broadcasted_iota(
        jnp.int32, (new_count, new_count), 1
    )
    ids_here = device_here * cand_here + lax.broadcasted_iota(jnp.int32, (cand_here,), 0)
    matched = kept[None, :] == ids_here[:, None]
    slot_index = jnp.sum(
        jnp.where(matched, lax.broadcasted_iota(jnp.int32, (cand_here, lane_number), 1), 0), axis=1
    )
    chosen = jnp.take(everyone, slot_index, axis=0)
    own_queries = chosen[:, :, : policy_heads * HD].reshape(
        cand_here, new_count, kv_here, policy_group, HD
    )
    own_fresh = chosen[:, :, policy_heads * HD :].reshape(cand_here, new_count, kv_here, 2 * HD)
    living = lax.broadcasted_iota(jnp.int32, (cand_here, cache_len), 1)
    living = living < jnp.take(extents, ids_here)[:, None]
    living = living[:, None, None, None, :]
    scores = (
        jnp.einsum("cikgd,ctkd->ckgit", own_queries, stored, preferred_element_type=f32)
        * key_scale
    )
    scores = jnp.where(living, scores, masked_value)
    fresh_scores = (
        jnp.einsum("cikgd,cjkd->ckgij", own_queries, own_fresh[..., :HD], preferred_element_type=f32)
        * key_scale
    )
    fresh_scores = jnp.where(causal_new, fresh_scores, masked_value)
    peak_score = jnp.maximum(jnp.max(scores, axis=-1), jnp.max(fresh_scores, axis=-1))
    old_weights = jnp.where(living, jnp.exp(scores - peak_score[..., None]), 0.0)
    fresh_weights = jnp.where(causal_new, jnp.exp(fresh_scores - peak_score[..., None]), 0.0)
    denominator = jnp.sum(old_weights, axis=-1) + jnp.sum(fresh_weights, axis=-1)
    numerator = jnp.einsum(
        "ckgit,ctkd->ckgid", old_weights, stored_values, preferred_element_type=f32
    )
    numerator = numerator + jnp.einsum(
        "ckgij,cjkd->ckgid", fresh_weights, own_fresh[..., HD:], preferred_element_type=f32
    )
    result = numerator / denominator[..., None]
    flattened = jnp.transpose(result, (0, 3, 1, 2, 4)).reshape(
        cand_here, new_count * policy_heads * HD
    )
    placed = jnp.einsum(
        "cs,cx->sx", matched.astype(f32), flattened, precision=lax.Precision.HIGHEST
    )
    return placed.reshape(lane_number, new_count, policy_heads * HD).astype(bf16)


def local(
    response_latest_embeddings,
    critic_probe_projector,
    critic_pair_projector,
    critic_stored_pairs,
    critic_grading_vector,
    actor_stored_pairs,
    filled_extents,
    kept_responses,
    actor_latest_probes,
    actor_latest_pairs,
):
    cand_here, span_len, _ = response_latest_embeddings.shape
    rows = cand_here * span_len
    devices = lax.axis_size("cand")
    group = lax.axis_index("groups")
    place = lax.axis_index("cand")
    depth, query_cols = critic_probe_projector.shape
    keyval_cols = critic_pair_projector.shape[1]
    heads_here = query_cols // HD
    per_group = heads_here // (keyval_cols // (2 * HD))
    query_half, keyval_half = query_cols // 2, keyval_cols // 2

    heads_half = heads_here // 2
    last = devices - 1
    tensor = lax.axis_size("tensor")

    def half_of(owner):
        pair = lax.dynamic_slice(critic_pair_projector, (0, owner * keyval_half), (depth, keyval_half))
        probe = lax.dynamic_slice(
            critic_probe_projector, (0, owner * query_half), (depth, query_half)
        )
        both = [pair[:, i : i + HD] for i in range(0, keyval_half, HD)]
        return both + [probe[:, i : i + HD] for i in range(0, query_half, HD)]

    mine, theirs = half_of(group), half_of(1 - group)
    count = len(mine)
    pairs = count - heads_half
    slots = jnp.concatenate([actor_latest_probes, actor_latest_pairs], axis=2)
    extra = slots.size // HD
    padding = -extra % 16
    mine[0] = jnp.concatenate([mine[0], slots.reshape(extra, HD), jnp.zeros((padding, HD), bf16)])
    value = {("w", 0, i): w for i, w in enumerate(mine)}
    value.update({("v", 0, i): w for i, w in enumerate(theirs)})

    value["token"] = jnp.zeros((8, HD), f32)

    def gate(*names):
        names = ["token"] + list(names)
        for name, array in zip(names, touch([value[n] for n in names])):
            value[name] = array

    each = range(cand_here)
    for c in each:
        value["own", 0, c] = response_latest_embeddings[c]
    bits = [1 << b for b in range(int(math.log2(tensor)) - 1, -1, -1)]
    held = [0]
    for bit in bits[:-1]:
        for off in list(held):
            for c in each:
                value["own", off ^ bit, c] = partner(value["own", off, c], "tensor", bit)
            held.append(off ^ bit)
    value["own", 1] = partner(response_latest_embeddings, "tensor", 1)

    wide = 2
    groups = [range(low, min(pairs, low + wide)) for low in range(0, pairs, wide)]
    groups += [range(low, min(count, low + wide)) for low in range(pairs, count, wide)]
    hops = [(step, i) for chosen in groups for step in range(last) for i in chosen]
    total = len(hops)
    extras = {}

    def at(number, *names):
        extras.setdefault(min(number, total + wide - 1), []).extend(names)

    def arrived(number):
        step, i = hops[number]
        return step + 1, i

    numbers = [(place - step) % devices for step in range(devices)]

    def multiply(begin, end, names, before, column, final):
        weights = [[value[side, step, i] for side, i in names] for step in range(begin, end)]
        pieces = [response_latest_embeddings, value["own", 1]]
        pieces += [[value["own", off, c] for c in each] for off in range(2, tensor)]
        done = project(pieces, numbers[begin:end], depth, weights, before, column, final)
        return done.reshape(rows, -1) if final else done

    grades = grading_columns(critic_grading_vector)
    value["share"] = jnp.zeros((cand_here, 8, span_len), f32)
    near = [off for off in held if off]
    def cross(c, until):
        for off in near:
            value["own", off ^ 1, c] = partner(value["own", off, c], "tensor", 1)
        at(until, *[("own", off ^ 1, c) for off in near])

    def policy_now():
        everyone = jnp.zeros((devices * slots.shape[0],) + slots.shape[1:], bf16)
        for step in range(devices):
            part = value["w", step, 0][depth : depth + extra].reshape(slots.shape)
            start = (place - step) % devices * slots.shape[0]
            everyone = lax.dynamic_update_slice(everyone, part, (start, 0, 0))
        value["policy"] = policy_rows(
            value["actor", 0], value["actor", 1], filled_extents, kept_responses, everyone
        )
        at(now + 3, "policy")

    def fresh_block(chunk):
        return jnp.where(chunk // pairs == group, 0, pairs) + chunk % pairs

    def score(queries, first_block, heads):
        owners = {"w": group, "v": 1 - group}
        numbers = [owners[side] * heads_half + i - pairs for side, i in heads]
        value["share"] = reward_share(
            queries,
            first_block,
            numbers,
            critic_stored_pairs,
            per_group,
            value["initial"],
            fresh_block,
            grades,
            value["share"],
        )

    def keyval_now():
        names = [(side, i) for side in "wv" for i in range(pairs)]
        value["initial"] = multiply(0, devices, names, None, 0, True)
        at(now + 1, "initial")

    def both(chosen):
        return [(side, i) for i in chosen for side in "wv"]

    def some_now(chosen, first, end):
        before = value.get(("sums", chosen))
        value["sums", chosen] = multiply(first, end, both(chosen), before, 0, False)
        at(min(now + 1, total + wide + lag - 1), ("sums", chosen))

    def queries_now(chosen, i):
        column = 2 * HD * chosen.index(i)
        before = value["sums", chosen]
        first = last if chosen is groups[-1] else min(2, last)
        value["queries", i] = multiply(first, devices, both([i]), before, column, True)
        at(now + 1, ("queries", i))

    def score_now(i):
        score(value["queries", i], 0, both([i]))
        at(now + 1, "share")

    def cache_now():
        value["actor", 0] = actor_stored_pairs[..., :HD]
        value["actor", 1] = actor_stored_pairs[..., HD:]
        at(now + 2, ("actor", 0), ("actor", 1))

    at(total + wide - 1, "policy")
    lag = 2

    def seen_at(step, i):
        return hops.index((step, i)) + wide + lag

    acts = [(seen_at(last - 1, 0) - lag, policy_now)]
    acts.append((seen_at(last - 1, pairs - 1), keyval_now))
    for chosen in groups:
        if chosen[0] < pairs:
            continue
        end = chosen[-1]
        ends = chosen is groups[-1]
        acts.append((seen_at(0, end) + ends, functools.partial(some_now, chosen, 0, 2)))
        if ends and last > 2:
            when = max(seen_at(0, end) + 2, seen_at(last - 2, end))
            acts.append((when, functools.partial(some_now, chosen, 2, last)))
        if chosen is not groups[-1]:
            for order, i in enumerate(chosen):
                when = seen_at(last - 1, i) + order
                acts.append((when, functools.partial(queries_now, chosen, i)))
                acts.append((when + 1, functools.partial(score_now, i)))
    acts.append((wide + 1, cache_now))
    for c in each:
        when = 7
        at(when, *[("own", off, c) for off in near])
        acts.append((when, functools.partial(cross, c, when + 2)))
    at(wide, ("own", 1))
    for now in range(total + wide + lag):
        names = []
        if 0 <= now - wide < total:
            names.append(("w",) + arrived(now - wide))
        if 0 <= now - wide - lag < total:
            names.append(("v",) + arrived(now - wide - lag))
        if now < total and hops[now][0] == 0 and now >= wide:
            names.append(("w",) + hops[now])
        names += extras.pop(now, [])
        if now >= wide:
            gate(*names)
        if now < total:
            step, i = hops[now]
            value["w", step + 1, i] = shifted(value["w", step, i], "cand", 1)
        if 0 <= now - wide < total:
            step, i = arrived(now - wide)
            value["v", step, i] = partner(value["w", step, i], "groups", 1)
        for when, act in acts:
            if when == now:
                act()

    chosen = groups[-1]
    for i in chosen:
        if i != chosen[0]:
            gate(("w", last, i), ("v", last, i), "share")
        queries_now(chosen, i)
        score_now(i)
    bit = devices // 2
    slot_rows = value["policy"]
    while bit:
        slot_rows = send_half(slot_rows, slots.shape[0], bit)
        bit //= 2
    share = value["share"]
    share = share[:, 0, :]
    terms = [share] + [partner(share, "tensor", bits) for bits in range(1, tensor)]
    while len(terms) > 1:
        terms = [a + b for a, b in zip(terms[::2], terms[1::2])]
    return terms[0], slot_rows


def solution(mesh):
    placed = (
        P(("groups", "cand"), None, "tensor"),
        P("cand", "tensor"),
        P("cand", "tensor"),
        P(("groups", "cand"), None, "tensor"),
        P("tensor"),
        P(("groups", "cand"), None, "tensor", None),
        P("groups"),
        P("groups"),
        P(("groups", "cand"), None, "tensor"),
        P(("groups", "cand"), None, "tensor"),
    )
    return jax.shard_map(
        local,
        mesh=mesh,
        in_specs=placed,
        out_specs=(P(("groups", "cand"), None), P(("groups", "cand"), None, "tensor")),
        check_vma=False,
    )
```

```python
import functools
import math

import jax
import jax.numpy as jnp
from jax import lax
from jax.experimental import pallas as pl
from jax.experimental.pallas import tpu as pltpu
from jax.sharding import PartitionSpec as P

HD = 128
masked_value = -1e30
bf16, f32 = jnp.bfloat16, jnp.float32


def touch(arrays):
    anywhere = pl.BlockSpec(memory_space=pl.ANY)
    return pl.pallas_call(
        lambda *refs: None,
        in_specs=[anywhere] * len(arrays),
        out_specs=[anywhere] * len(arrays),
        out_shape=[jax.ShapeDtypeStruct(v.shape, v.dtype) for v in arrays],
        input_output_aliases={i: i for i in range(len(arrays))},
        compiler_params=pltpu.CompilerParams(vmem_limit_bytes=60 * 1024 * 1024),
        cost_estimate=pl.CostEstimate(flops=0, bytes_accessed=0, transcendentals=0),
        name="touch",
    )(*arrays)


def shifted(value, axis, step):
    size = lax.axis_size(axis)
    return lax.ppermute(value, axis, [(i, (i + step) % size) for i in range(size)])


def partner(value, axis, bits):
    size = lax.axis_size(axis)
    return lax.ppermute(value, axis, [(i, i ^ bits) for i in range(size)])


def project_kernel(plan, where_ref, *refs):
    sources, tile_of, blocks, widths, begin, has_sum = plan
    arrays, refs = refs[:sources], refs[sources:]
    cands = len(tile_of[0])
    weights, refs = refs[: blocks * len(widths)], refs[blocks * len(widths) :]
    before, refs = (refs[0], refs[1:]) if has_sum else (None, refs)
    out, tile_buf, weight_buf, sum_buf, tile_sem, weight_sem, sum_sem = refs
    slots, tile_rows, depth = tile_buf.shape
    columns = sum_buf.shape[2]
    steps = cands * blocks

    def load(item):
        block, tile = item // cands, item % cands
        off, column = where_ref[2 * block], where_ref[2 * block + 1]
        column = pl.multiple_of(column, depth)
        slot = lax.rem(item, slots)
        for i, row in enumerate(tile_of):
            for j, (number, place) in enumerate(row):

                @pl.when((off == i) & (tile == j))
                def _():
                    whole = arrays[number] if place is None else arrays[number].at[place]
                    pltpu.make_async_copy(
                        whole.at[:, pl.ds(column, depth)], tile_buf.at[slot], tile_sem.at[slot]
                    ).start()

    copies = []
    for block in range(blocks):
        at = 0
        copies.append([])
        for j, width in enumerate(widths):
            number = block * len(widths) + j
            copies[-1].append(
                pltpu.make_async_copy(
                    weights[number].at[0:depth, :],
                    weight_buf.at[block, :, at : at + width],
                    weight_sem.at[number],
                )
            )
            at += width
    for copy in copies[0]:
        copy.start()
    for item in range(min(slots - 1, steps)):
        load(item)
    if has_sum:
        columns_of = before.at[:, :, begin : begin + columns]
        sum_copy = pltpu.make_async_copy(columns_of, sum_buf, sum_sem)
        sum_copy.start()
    for block in copies[1:]:
        for copy in block:
            copy.start()

    def step(item, _):
        @pl.when(item + slots - 1 < steps)
        def _():
            load(item + slots - 1)

        slot = lax.rem(item, slots)
        block, tile = item // cands, item % cands
        for i in range(blocks):

            @pl.when(item == i * cands)
            def _():
                for copy in copies[i]:
                    copy.wait()

        if has_sum:

            @pl.when(item == 0)
            def _():
                sum_copy.wait()

        pltpu.make_async_copy(
            arrays[0].at[0, :, pl.ds(0, depth)] if tile_of[0][0][1] is not None else arrays[0].at[:, pl.ds(0, depth)],
            tile_buf.at[slot],
            tile_sem.at[slot],
        ).wait()
        term = jnp.dot(tile_buf[slot], weight_buf[block], preferred_element_type=f32)
        if has_sum:
            term = term + sum_buf[tile]
        else:
            term = jnp.where(block > 0, term + sum_buf[tile], term)
        if blocks > 1:
            sum_buf[tile] = term

        @pl.when(block == blocks - 1)
        def _():
            out[tile] = term.astype(out.dtype)

        return 0

    lax.fori_loop(0, steps, step, 0)


def project(pieces, numbers, depth, weights, before, begin, final):
    here = lax.axis_index("tensor")
    cands, tile_rows, width = pieces[0].shape
    arrays, tile_of = [], []
    for piece in pieces:
        if isinstance(piece, list):
            tile_of.append([(len(arrays) + c, None) for c in range(cands)])
            arrays += piece
        else:
            tile_of.append([(len(arrays), c) for c in range(cands)])
            arrays.append(piece)
    blocks = len(weights)
    widths = [w.shape[1] for w in weights[0]]
    columns = sum(widths)
    per_piece = width // depth
    where = []
    for number in numbers:
        where += [(number // per_piece) ^ here, number % per_piece * depth]
    where = jnp.stack(where).astype(jnp.int32)
    flat = [w for block in weights for w in block]
    operands = arrays + flat + ([] if before is None else [before])
    plan = (len(arrays), tile_of, blocks, widths, begin, before is not None)
    slots = 3
    return pl.pallas_call(
        functools.partial(project_kernel, plan),
        in_specs=[pl.BlockSpec(memory_space=pltpu.SMEM)]
        + [pl.BlockSpec(memory_space=pl.ANY)] * len(operands),
        out_specs=pl.BlockSpec(memory_space=pltpu.VMEM),
        out_shape=jax.ShapeDtypeStruct((cands, tile_rows, columns), bf16 if final else f32),
        scratch_shapes=[
            pltpu.VMEM((slots, tile_rows, depth), bf16),
            pltpu.VMEM((blocks, depth, columns), bf16),
            pltpu.VMEM((cands, tile_rows, columns), f32),
            pltpu.SemaphoreType.DMA((slots,)),
            pltpu.SemaphoreType.DMA((len(flat),)),
            pltpu.SemaphoreType.DMA,
        ],
        compiler_params=pltpu.CompilerParams(vmem_limit_bytes=60 * 1024 * 1024),
        cost_estimate=pl.CostEstimate(
            flops=2 * cands * tile_rows * depth * blocks * columns,
            bytes_accessed=2 * cands * tile_rows * depth * blocks,
            transcendentals=0,
        ),
        name="project",
    )(where, *operands)


def reward_kernel(kg_ref, q_ref, old_key_ref, old_value_ref, key_ref, value_ref, grade_ref, so_far_ref, out_ref):
    span = q_ref.shape[0]
    context = old_key_ref.shape[1]
    rate = HD**-0.5 * math.log2(math.e)
    queries = q_ref[...]
    grade = grade_ref[0]
    block = math.gcd(HD, context)
    peak = jnp.full((8, span), -jnp.inf, f32)
    total = jnp.zeros((8, span), f32)
    graded = jnp.zeros((8, span), f32)
    places = [(old_key_ref.at[0], old_value_ref.at[0], i) for i in range(0, context, block)]
    places += [(key_ref, value_ref, i) for i in range(0, span, block)]

    def products(keys, values, start):
        scores = lax.dot_general(
            keys[start : start + block, :],
            queries,
            (((1,), (1,)), ((), ())),
            preferred_element_type=f32,
        )
        worth = jnp.dot(values[start : start + block, :], grade, preferred_element_type=f32)
        worth = worth[:, :HD] + worth[:, HD:]
        if keys is key_ref:
            shape = (block, span)
            visible = start + lax.broadcasted_iota(jnp.int32, shape, 0) <= (
                lax.broadcasted_iota(jnp.int32, shape, 1)
            )
            scores = jnp.where(visible, scores, masked_value)
        return scores.reshape(block // 8, 8, span), worth.reshape(block // 8, 8, HD)

    coming = products(*places[0])
    for number in range(len(places)):
        scores, worth = coming
        if number + 1 < len(places):
            coming = products(*places[number + 1])
        new_peak = jnp.maximum(peak, jnp.max(scores, axis=0))
        fade = jnp.exp2((peak - new_peak) * rate)
        weights = jnp.exp2((scores - new_peak[None]) * rate)
        total = total * fade + jnp.sum(weights, axis=0)
        worth = jnp.concatenate([worth] * (span // HD), axis=2)
        graded = graded * fade + jnp.sum(weights * worth, axis=0)
        peak = new_peak
    top = jnp.max(peak, axis=0, keepdims=True)
    fade = jnp.exp2((peak - top) * rate)
    total = jnp.sum(total * fade, axis=0, keepdims=True)
    graded = jnp.sum(graded * fade, axis=0, keepdims=True)
    result = jnp.broadcast_to(graded / total, (8, span))

    @pl.when(pl.program_id(1) == 0)
    def _():
        out_ref[0] = so_far_ref[0] + result

    @pl.when(pl.program_id(1) != 0)
    def _():
        out_ref[0] += result


def grading_columns(grading):
    high = lax.reduce_precision(grading, 8, 7)
    parts = []
    for part in (high, grading - high):
        part = part.astype(bf16).reshape(-1, HD)
        parts.append(jnp.broadcast_to(part[:, :, None], (part.shape[0], HD, HD)))
    return jnp.concatenate(parts, axis=2)


def reward_share(queries, first_block, numbers, stored, per_group, fresh, fresh_block, grades, so_far):
    cands, context, _ = stored.shape
    span = queries.shape[0] // cands
    heads = len(numbers)
    scalars = []
    for number in numbers:
        pair = number // per_group
        scalars += [number, 2 * pair, fresh_block(2 * pair), fresh_block(2 * pair + 1)]
    scalars = jnp.stack(scalars).astype(jnp.int32)
    spec = pltpu.PrefetchScalarGridSpec(
        num_scalar_prefetch=1,
        grid=(cands, heads),
        in_specs=[
            pl.BlockSpec((span, HD), lambda c, h, n: (c, first_block + h)),
            pl.BlockSpec((1, context, HD), lambda c, h, n: (c, 0, n[4 * h + 1])),
            pl.BlockSpec((1, context, HD), lambda c, h, n: (c, 0, n[4 * h + 1] + 1)),
            pl.BlockSpec((span, HD), lambda c, h, n: (c, n[4 * h + 2])),
            pl.BlockSpec((span, HD), lambda c, h, n: (c, n[4 * h + 3])),
            pl.BlockSpec((1, HD, 2 * HD), lambda c, h, n: (n[4 * h], 0, 0)),
            pl.BlockSpec((1, 8, span), lambda c, h, n: (c, 0, 0)),
        ],
        out_specs=pl.BlockSpec((1, 8, span), lambda c, h, n: (c, 0, 0)),
    )
    cells = cands * heads * span * (context + span)
    return pl.pallas_call(
        reward_kernel,
        grid_spec=spec,
        out_shape=jax.ShapeDtypeStruct((cands, 8, span), f32),
        compiler_params=pltpu.CompilerParams(vmem_limit_bytes=60 * 1024 * 1024),
        cost_estimate=pl.CostEstimate(
            flops=6 * HD * cells, bytes_accessed=4 * stored.size, transcendentals=cells
        ),
        name="reward_share",
    )(scalars, queries, stored, stored, fresh, fresh, grades, so_far)


def send_half(placed, slots_here, bit):
    low = (lax.axis_index("cand") & bit) == 0
    first, second = placed[: bit * slots_here], placed[bit * slots_here :]
    new = partner(jnp.where(low, second, first), "cand", bit)
    return jnp.where(low, first, second) + new


def policy_rows(stored, stored_values, extents, kept, everyone):
    cand_here = stored.shape[0]
    device_here = lax.axis_index("cand")
    key_scale = HD ** (-0.5)
    lane_number = kept.shape[0]
    new_count = everyone.shape[1]
    kv_here = stored.shape[2]
    policy_heads = everyone.shape[2] // HD - 2 * kv_here
    policy_group = policy_heads // kv_here
    cache_len = stored.shape[1]
    causal_new = lax.broadcasted_iota(jnp.int32, (new_count, new_count), 0) >= lax.broadcasted_iota(
        jnp.int32, (new_count, new_count), 1
    )
    ids_here = device_here * cand_here + lax.broadcasted_iota(jnp.int32, (cand_here,), 0)
    matched = kept[None, :] == ids_here[:, None]
    slot_index = jnp.sum(
        jnp.where(matched, lax.broadcasted_iota(jnp.int32, (cand_here, lane_number), 1), 0), axis=1
    )
    chosen = jnp.take(everyone, slot_index, axis=0)
    own_queries = chosen[:, :, : policy_heads * HD].reshape(
        cand_here, new_count, kv_here, policy_group, HD
    )
    own_fresh = chosen[:, :, policy_heads * HD :].reshape(cand_here, new_count, kv_here, 2 * HD)
    living = lax.broadcasted_iota(jnp.int32, (cand_here, cache_len), 1)
    living = living < jnp.take(extents, ids_here)[:, None]
    living = living[:, None, None, None, :]
    scores = (
        jnp.einsum("cikgd,ctkd->ckgit", own_queries, stored, preferred_element_type=f32)
        * key_scale
    )
    scores = jnp.where(living, scores, masked_value)
    fresh_scores = (
        jnp.einsum("cikgd,cjkd->ckgij", own_queries, own_fresh[..., :HD], preferred_element_type=f32)
        * key_scale
    )
    fresh_scores = jnp.where(causal_new, fresh_scores, masked_value)
    peak_score = jnp.maximum(jnp.max(scores, axis=-1), jnp.max(fresh_scores, axis=-1))
    old_weights = jnp.where(living, jnp.exp(scores - peak_score[..., None]), 0.0)
    fresh_weights = jnp.where(causal_new, jnp.exp(fresh_scores - peak_score[..., None]), 0.0)
    denominator = jnp.sum(old_weights, axis=-1) + jnp.sum(fresh_weights, axis=-1)
    numerator = jnp.einsum(
        "ckgit,ctkd->ckgid", old_weights, stored_values, preferred_element_type=f32
    )
    numerator = numerator + jnp.einsum(
        "ckgij,cjkd->ckgid", fresh_weights, own_fresh[..., HD:], preferred_element_type=f32
    )
    result = numerator / denominator[..., None]
    flattened = jnp.transpose(result, (0, 3, 1, 2, 4)).reshape(
        cand_here, new_count * policy_heads * HD
    )
    placed = jnp.einsum(
        "cs,cx->sx", matched.astype(f32), flattened, precision=lax.Precision.HIGHEST
    )
    return placed.reshape(lane_number, new_count, policy_heads * HD).astype(bf16)


def local(
    response_latest_embeddings,
    critic_probe_projector,
    critic_pair_projector,
    critic_stored_pairs,
    critic_grading_vector,
    actor_stored_pairs,
    filled_extents,
    kept_responses,
    actor_latest_probes,
    actor_latest_pairs,
):
    cand_here, span_len, _ = response_latest_embeddings.shape
    rows = cand_here * span_len
    devices = lax.axis_size("cand")
    group = lax.axis_index("groups")
    place = lax.axis_index("cand")
    depth, query_cols = critic_probe_projector.shape
    keyval_cols = critic_pair_projector.shape[1]
    heads_here = query_cols // HD
    per_group = heads_here // (keyval_cols // (2 * HD))
    query_half, keyval_half = query_cols // 2, keyval_cols // 2

    heads_half = heads_here // 2
    last = devices - 1
    tensor = lax.axis_size("tensor")

    def half_of(owner):
        pair = lax.dynamic_slice(critic_pair_projector, (0, owner * keyval_half), (depth, keyval_half))
        probe = lax.dynamic_slice(
            critic_probe_projector, (0, owner * query_half), (depth, query_half)
        )
        both = [pair[:, i : i + HD] for i in range(0, keyval_half, HD)]
        return both + [probe[:, i : i + HD] for i in range(0, query_half, HD)]

    mine, theirs = half_of(group), half_of(1 - group)
    count = len(mine)
    pairs = count - heads_half
    slots = jnp.concatenate([actor_latest_probes, actor_latest_pairs], axis=2)
    extra = slots.size // HD
    padding = -extra % 16
    mine[0] = jnp.concatenate([mine[0], slots.reshape(extra, HD), jnp.zeros((padding, HD), bf16)])
    value = {("w", 0, i): w for i, w in enumerate(mine)}
    value.update({("v", 0, i): w for i, w in enumerate(theirs)})

    value["token"] = jnp.zeros((8, HD), f32)

    def gate(*names):
        names = ["token"] + list(names)
        for name, array in zip(names, touch([value[n] for n in names])):
            value[name] = array

    each = range(cand_here)
    for c in each:
        value["own", 0, c] = response_latest_embeddings[c]
    bits = [1 << b for b in range(int(math.log2(tensor)) - 1, -1, -1)]
    held = [0]
    for bit in bits[:-1]:
        for off in list(held):
            for c in each:
                value["own", off ^ bit, c] = partner(value["own", off, c], "tensor", bit)
            held.append(off ^ bit)
    value["own", 1] = partner(response_latest_embeddings, "tensor", 1)

    wide = 2
    groups = [range(low, min(pairs, low + wide)) for low in range(0, pairs, wide)]
    groups += [range(low, min(count, low + wide)) for low in range(pairs, count, wide)]
    hops = [(step, i) for chosen in groups for step in range(last) for i in chosen]
    total = len(hops)
    extras = {}

    def at(number, *names):
        extras.setdefault(min(number, total + wide - 1), []).extend(names)

    def arrived(number):
        step, i = hops[number]
        return step + 1, i

    numbers = [(place - step) % devices for step in range(devices)]

    def multiply(begin, end, names, before, column, final):
        weights = [[value[side, step, i] for side, i in names] for step in range(begin, end)]
        pieces = [response_latest_embeddings, value["own", 1]]
        pieces += [[value["own", off, c] for c in each] for off in range(2, tensor)]
        done = project(pieces, numbers[begin:end], depth, weights, before, column, final)
        return done.reshape(rows, -1) if final else done

    grades = grading_columns(critic_grading_vector)
    value["share"] = jnp.zeros((cand_here, 8, span_len), f32)
    near = [off for off in held if off]
    def cross(c, until):
        for off in near:
            value["own", off ^ 1, c] = partner(value["own", off, c], "tensor", 1)
        at(until, *[("own", off ^ 1, c) for off in near])

    def policy_now():
        everyone = jnp.zeros((devices * slots.shape[0],) + slots.shape[1:], bf16)
        for step in range(devices):
            part = value["w", step, 0][depth : depth + extra].reshape(slots.shape)
            start = (place - step) % devices * slots.shape[0]
            everyone = lax.dynamic_update_slice(everyone, part, (start, 0, 0))
        value["policy"] = policy_rows(
            value["actor", 0], value["actor", 1], filled_extents, kept_responses, everyone
        )
        at(now + 3, "policy")

    def fresh_block(chunk):
        return jnp.where(chunk // pairs == group, 0, pairs) + chunk % pairs

    def score(queries, first_block, heads):
        owners = {"w": group, "v": 1 - group}
        numbers = [owners[side] * heads_half + i - pairs for side, i in heads]
        value["share"] = reward_share(
            queries,
            first_block,
            numbers,
            critic_stored_pairs,
            per_group,
            value["initial"],
            fresh_block,
            grades,
            value["share"],
        )

    def keyval_now():
        names = [(side, i) for side in "wv" for i in range(pairs)]
        value["initial"] = multiply(0, devices, names, None, 0, True)
        at(now + 1, "initial")

    def both(chosen):
        return [(side, i) for i in chosen for side in "wv"]

    def some_now(chosen, first, end):
        before = value.get(("sums", chosen))
        value["sums", chosen] = multiply(first, end, both(chosen), before, 0, False)
        at(min(now + 1, total + wide + lag - 1), ("sums", chosen))

    def queries_now(chosen, i):
        column = 2 * HD * chosen.index(i)
        before = value["sums", chosen]
        first = last if chosen is groups[-1] else min(2, last)
        value["queries", i] = multiply(first, devices, both([i]), before, column, True)
        at(now + 1, ("queries", i))

    def score_now(i):
        score(value["queries", i], 0, both([i]))
        at(now + 1, "share")

    def cache_now():
        value["actor", 0] = actor_stored_pairs[..., :HD]
        value["actor", 1] = actor_stored_pairs[..., HD:]
        at(now + 2, ("actor", 0), ("actor", 1))

    at(total + wide - 1, "policy")
    lag = 2

    def seen_at(step, i):
        return hops.index((step, i)) + wide + lag

    acts = [(seen_at(last - 1, 0) - lag, policy_now)]
    acts.append((seen_at(last - 1, pairs - 1), keyval_now))
    for chosen in groups:
        if chosen[0] < pairs:
            continue
        end = chosen[-1]
        ends = chosen is groups[-1]
        acts.append((seen_at(0, end) + ends, functools.partial(some_now, chosen, 0, 2)))
        if ends and last > 2:
            when = max(seen_at(0, end) + 2, seen_at(last - 2, end))
            acts.append((when, functools.partial(some_now, chosen, 2, last)))
        if chosen is not groups[-1]:
            for order, i in enumerate(chosen):
                when = seen_at(last - 1, i) + order
                acts.append((when, functools.partial(queries_now, chosen, i)))
                acts.append((when + 1, functools.partial(score_now, i)))
    acts.append((wide + 1, cache_now))
    for c in each:
        when = 6 + c
        at(when, *[("own", off, c) for off in near])
        acts.append((when, functools.partial(cross, c, 9)))
    at(wide, ("own", 1))
    for now in range(total + wide + lag):
        names = []
        if 0 <= now - wide < total:
            names.append(("w",) + arrived(now - wide))
        if 0 <= now - wide - lag < total:
            names.append(("v",) + arrived(now - wide - lag))
        if now < total and hops[now][0] == 0 and now >= wide:
            names.append(("w",) + hops[now])
        names += extras.pop(now, [])
        if now >= wide:
            gate(*names)
        if now < total:
            step, i = hops[now]
            value["w", step + 1, i] = shifted(value["w", step, i], "cand", 1)
        if 0 <= now - wide < total:
            step, i = arrived(now - wide)
            value["v", step, i] = partner(value["w", step, i], "groups", 1)
        for when, act in acts:
            if when == now:
                act()

    chosen = groups[-1]
    for i in chosen:
        if i != chosen[0]:
            gate(("w", last, i), ("v", last, i), "share")
        queries_now(chosen, i)
        score_now(i)
    bit = devices // 2
    slot_rows = value["policy"]
    while bit:
        slot_rows = send_half(slot_rows, slots.shape[0], bit)
        bit //= 2
    share = value["share"]
    share = share[:, 0, :]
    terms = [share] + [partner(share, "tensor", bits) for bits in range(1, tensor)]
    while len(terms) > 1:
        terms = [a + b for a, b in zip(terms[::2], terms[1::2])]
    return terms[0], slot_rows


def solution(mesh):
    placed = (
        P(("groups", "cand"), None, "tensor"),
        P("cand", "tensor"),
        P("cand", "tensor"),
        P(("groups", "cand"), None, "tensor"),
        P("tensor"),
        P(("groups", "cand"), None, "tensor", None),
        P("groups"),
        P("groups"),
        P(("groups", "cand"), None, "tensor"),
        P(("groups", "cand"), None, "tensor"),
    )
    return jax.shard_map(
        local,
        mesh=mesh,
        in_specs=placed,
        out_specs=(P(("groups", "cand"), None), P(("groups", "cand"), None, "tensor")),
        check_vma=False,
    )
```
